128 devices in a mesh: blk: 32 (over x, y, core), uly: 4 (over z).
Axes of the slice: x: 4, y: 4, z: 4, core: 2. Of those that a mesh axis runs over, the one named last changes fastest.
Arguments:
- queries: bfloat16 [16384, 4096], P(('blk', 'uly')), may hold values from -100 to 100
- keys: bfloat16 [16384, 512], P(('blk', 'uly')), may hold values from -6 to 6
- values: bfloat16 [16384, 512], P(('blk', 'uly')), may hold values from -6 to 6
- segments: int32 [16384], P(('blk', 'uly')), may hold values from 0 to 7, never falling along the last dimension, each value on 1 to 8192 neighbouring positions
Outputs:
- attended: bfloat16 [16384, 4096], P(('blk', 'uly'))
The draws below stay inside these ranges and needn't reach their ends.
Inputs may be any that keep to these rules, and one draw needn't show every extreme that they name: `segments`: document numbers never fall along the sequence; each document holds 1 to 8192 positions.
All inputs are finite; a program needn't handle non-finite values.
Results may differ from the reference program's by a relative error of at most 0.0039.
Values may be sent and summed in bfloat16 or wider, within the bound.
A program may use at most 64 MiB of HBM per device.

```python
import math
import jax
import jax.numpy as jnp
import numpy as np
from jax import lax

QUERY_HEADS = 32
KEY_VALUE_HEADS = 4
HEAD_SIZE = 128
NDOC = 8
SEQUENCE_LENGTH = 16384


def shared_pair(key):
    base_offset = jax.random.fold_in(key, 7)
    key_subset = jnp.clip(jax.random.normal(jax.random.fold_in(base_offset, 1), (SEQUENCE_LENGTH, KEY_VALUE_HEADS * HEAD_SIZE), jnp.float32), -6.0, 6.0)
    queryset = jnp.clip(jax.random.normal(jax.random.fold_in(base_offset, 2), (SEQUENCE_LENGTH, QUERY_HEADS * HEAD_SIZE), jnp.float32), -6.0, 6.0)
    return (queryset, key_subset)


def draw_queries(key, part):
    return shared_pair(key)[0].astype(jnp.bfloat16)


def draw_keys(key, part):
    return shared_pair(key)[1].astype(jnp.bfloat16)


def levels(stream_key, shape, shards, least, top_value):
    def one(axis_at, shards_of):
        draws = jax.random.uniform(jax.random.fold_in(jax.random.fold_in(stream_key, 6), axis_at), (shards_of,), jnp.float32, least / len(shards), top_value / len(shards))
        return jnp.repeat(jnp.exp(draws), shape[axis_at] // shards_of).reshape((-1,) + (1,) * (len(shape) - axis_at - 1))

    loudness = one(*shards[0])
    for cut in shards[1:]:
        loudness = loudness * one(*cut)
    return loudness


def split_up(number_of, total, reach, lean):
    loads = [(1 << 20) // math.isqrt(standing ** lean) + 1 for standing in range(2, number_of + 1)]
    spare, given = total - reach - (number_of - 1), [1] * (number_of - 1)
    while spare > 0:
        movable = [i for i in range(number_of - 1) if given[i] < reach]
        pool, budget = sum([loads[i] for i in movable]), spare
        for i in movable:
            addition = min(reach - given[i], max(1, budget * loads[i] // pool), spare)
            given[i] = given[i] + addition
            spare = spare - addition
    return np.array([reach] + given)


def uneven(key, amount, total, bound, slope):
    if amount == 2:
        one = jax.random.randint(key, (), max(1, total - bound), min(bound, total - 1) + 1)
        return jnp.stack([one, total - one])
    tallies = jnp.asarray(split_up(amount, total, bound, slope), jnp.int32)
    twos = (amount - 1) // 2
    source_of, sink = tallies[1:1 + 2 * twos:2], tallies[2:2 + 2 * twos:2]
    room = jnp.minimum(source_of - 1, bound - sink)
    moved = jax.random.randint(jax.random.fold_in(key, 1), (twos,), 0, 1 << 20) % (room + 1)
    tallies = tallies.at[1:1 + 2 * twos:2].set(source_of - moved).at[2:2 + 2 * twos:2].set(sink + moved)
    return tallies[jax.random.permutation(jax.random.fold_in(key, 2), amount)]


def centred(own_key, extent, deviation, most, cuts=(), held_as=jnp.bfloat16):
    entries = jax.random.normal(own_key, extent, jnp.float32) * deviation
    if len(cuts) > 0:
        entries = levels(own_key, extent, cuts, -0.22, 0.18) * entries
    return jnp.clip(entries, min=-most, max=most).astype(held_as)


def setup_inputs(seed: int = 0) -> dict:
    key_list = jax.random.split(jax.random.key(seed), 5)
    queries = draw_queries(jax.random.fold_in(key_list[4], 71), 0)
    keys = draw_keys(jax.random.fold_in(key_list[4], 71), 0)
    values = centred(key_list[2], (SEQUENCE_LENGTH, KEY_VALUE_HEADS * HEAD_SIZE), 1.0, 6.0, ((0, 128),))
    segments = jnp.searchsorted(jnp.cumsum(uneven(key_list[3], NDOC, SEQUENCE_LENGTH, SEQUENCE_LENGTH // 2, 2)), jnp.arange(SEQUENCE_LENGTH), side="right").astype(jnp.int32)
    return {"queries": queries, "keys": keys, "values": values, "segments": segments}


def reference(queries, keys, values, segments):
    span_length = queries.shape[0]
    head_groups = QUERY_HEADS // KEY_VALUE_HEADS
    block = min(512, span_length)
    count = span_length // block
    scale = HEAD_SIZE ** -0.5
    query_rows = queries.reshape(span_length, KEY_VALUE_HEADS, head_groups, HEAD_SIZE)
    key_rows = keys.reshape(span_length, KEY_VALUE_HEADS, HEAD_SIZE)
    value_rows = values.reshape(span_length, KEY_VALUE_HEADS, HEAD_SIZE)
    places = jnp.arange(span_length, dtype=jnp.int32)

    def single_head(head):
        qhead = query_rows[:, head]
        khead = key_rows[:, head].astype(jnp.float32)
        vhead = value_rows[:, head].astype(jnp.float32)

        def one_block(index):
            first = (index * block).astype(jnp.int32)
            qblk = lax.dynamic_slice_in_dim(qhead, first, block, 0).astype(jnp.float32)
            qpos = first + jnp.arange(block, dtype=jnp.int32)
            qseg = lax.dynamic_slice_in_dim(segments, first, block, 0)
            scores = jnp.einsum("qgd,kd->gqk", qblk, khead) * scale
            allowed = (places[None, :] <= qpos[:, None]) & (segments[None, :] == qseg[:, None])
            scores = jnp.where(allowed[None], scores, -1e30)
            top = jnp.max(scores, axis=-1, keepdims=True)
            probs = jnp.where(allowed[None], jnp.exp(scores - top), 0.0)
            total = jnp.sum(probs, axis=-1)
            rounded = lax.optimization_barrier(probs.astype(jnp.bfloat16)).astype(jnp.float32)
            summed = jnp.einsum("gqk,kd->qgd", rounded, vhead)
            return summed / jnp.transpose(total)[:, :, None]

        return lax.map(one_block, jnp.arange(count, dtype=jnp.int32))

    final_output = lax.map(single_head, jnp.arange(KEY_VALUE_HEADS, dtype=jnp.int32))
    final_output = jnp.transpose(final_output, (1, 2, 0, 3, 4)).reshape(span_length, QUERY_HEADS * HEAD_SIZE)
    return final_output.astype(jnp.bfloat16)
```

```python
import functools
import jax, jax.numpy as jnp
from jax import lax
from jax.experimental import pallas as pl
from jax.experimental.pallas import tpu as pltpu
from jax.sharding import Mesh
from jax.sharding import PartitionSpec as P

HEAD_SIZE = 128
NDOC = 8
GROUP = 8
SCALE2 = 1.4426950408889634 * HEAD_SIZE ** -0.5
ONES = 16
UNIT = 512
BIG = 2048


def doc_start(info, pos):
    low = jnp.zeros_like(pos)
    for d in range(1, NDOC):
        low = jnp.where(info[d] <= pos, jnp.maximum(low, info[d]), low)
    return low


def contract(a, b, da, db):
    return lax.dot_general(a, b, (((da,), (db,)), ((), ())), preferred_element_type=jnp.float32)


def attend(info, q_ref, k_hbm, v_hbm, o_ref, kbuf, vbuf, qcat, acc, top, sems):
    D = HEAD_SIZE
    tiles, pieces, piece, _ = q_ref.shape
    rows = pieces * piece
    M = GROUP * rows
    part = kbuf.shape[0] // tiles
    shard = UNIT // pieces

    def loads(t):
        at = pl.ds(t * part, part)
        return (
            pltpu.make_async_copy(k_hbm.at[at], kbuf.at[at], sems.at[0, t]),
            pltpu.make_async_copy(v_hbm.at[at], vbuf.at[at], sems.at[1, t]),
        )

    for t in range(tiles):
        for c in loads(t):
            c.start()

    @pl.loop(0, tiles)
    def _(t):
        base = info[NDOC] + t * part
        first = base + info[NDOC + 1]
        last = first + (pieces - 1) * shard + piece - 1
        for c in loads(t):
            c.wait()
        low = doc_start(info, first) // UNIT
        diag = base // UNIT
        lane = lax.broadcasted_iota(jnp.int32, (1, rows), 1)
        qpos = first + (lane // piece) * shard + lane % piece
        qlow = doc_start(info, qpos)

        for g in range(GROUP):
            q = q_ref[t, :, :, g * D:(g + 1) * D].reshape(rows, D).astype(jnp.float32) * SCALE2
            high = q.astype(jnp.bfloat16)
            at = slice(g * rows, (g + 1) * rows)
            qcat[at, :D] = high
            qcat[at, D:] = (q - high.astype(jnp.float32)).astype(jnp.bfloat16)
        acc[...] = jnp.zeros_like(acc)

        def allowed(at, size):
            kpos = at + lax.broadcasted_iota(jnp.int32, (size, rows), 0)
            return (kpos <= qpos) & (kpos >= qlow)

        def masked(p, m):
            return jnp.concatenate(
                [jnp.where(m, p[:, g * rows:(g + 1) * rows], 0.0) for g in range(p.shape[1] // rows)], axis=1)

        def step(at, size):
            at = pl.multiple_of(at, UNIT)
            k = kbuf[pl.ds(at, size), :]
            v = vbuf[pl.ds(at, size), :]
            kk = jnp.concatenate([k, k], axis=1)
            vv = jnp.concatenate([v, jnp.ones((size, ONES), v.dtype)], axis=1)
            p = masked(jnp.exp2(contract(kk, qcat[...], 1, 1)), allowed(at, size))
            acc[...] += contract(vv, p.astype(jnp.bfloat16), 0, 0)

        end = (diag + 1) * UNIT
        units = diag + 1 - low
        per = BIG // UNIT
        big = units // per
        begin = low * UNIT

        @pl.loop(0, big)
        def _(n):
            step(begin + n * BIG, BIG)

        size = BIG // 2
        done = big * BIG
        while size >= UNIT:
            some = (units // (size // UNIT)) % 2

            @pl.when(some == 1)
            def _(done=done, size=size):
                step(begin + done, size)

            done = done + some * size
            size //= 2

        total = acc[D:D + 8, :]
        good = jnp.min(jnp.where((total > 2.0 ** -60) & (total < 2.0 ** 118), 1.0, 0.0))

        @pl.when(good < 0.5)
        def _():
            top[...] = jnp.full_like(top, -1e30)
            acc[...] = jnp.zeros_like(acc)

            def scores(n, g):
                at = pl.multiple_of(n * UNIT, UNIT)
                q = q_ref[t, :, :, pl.ds(pl.multiple_of(g * D, D), D)].reshape(rows, D)
                m = allowed(at, UNIT)
                return jnp.where(m, contract(kbuf[pl.ds(at, UNIT), :], q, 1, 1) * SCALE2, -1e30), m

            @pl.loop(low, diag + 1)
            def _(n):
                @pl.loop(0, GROUP)
                def _(g):
                    at = pl.ds(pl.multiple_of(g * rows, rows), rows)
                    s, _ = scores(n, g)
                    top[:, at] = jnp.maximum(top[:, at], jnp.max(s, axis=0, keepdims=True))

            @pl.loop(low, diag + 1)
            def _(n):
                v = vbuf[pl.ds(pl.multiple_of(n * UNIT, UNIT), UNIT), :]
                vv = jnp.concatenate([v, jnp.ones((UNIT, ONES), v.dtype)], axis=1)

                @pl.loop(0, GROUP)
                def _(g):
                    at = pl.ds(pl.multiple_of(g * rows, rows), rows)
                    s, m = scores(n, g)
                    p = jnp.where(m, jnp.exp2(s - top[:1, at]), 0.0)
                    acc[:, at] += contract(vv, p.astype(jnp.bfloat16), 0, 0)

        for g in range(GROUP):
            at = slice(g * rows, (g + 1) * rows)
            out = acc[:D, at] / acc[D:D + 1, at]
            o_ref[t, :, :, g * D:(g + 1) * D] = out.T.astype(jnp.bfloat16).reshape(pieces, piece, D)


def attention(info, q, k, v):
    tiles, pieces, piece, width = q.shape
    M = GROUP * pieces * piece
    vm = pl.BlockSpec(memory_space=pltpu.VMEM)
    anywhere = pl.BlockSpec(memory_space=pl.ANY)
    return pl.pallas_call(
        attend,
        out_shape=jax.ShapeDtypeStruct(q.shape, jnp.bfloat16),
        in_specs=[pl.BlockSpec(memory_space=pltpu.SMEM), vm, anywhere, anywhere],
        out_specs=vm,
        scratch_shapes=[
            pltpu.VMEM(k.shape, jnp.bfloat16),
            pltpu.VMEM(v.shape, jnp.bfloat16),
            pltpu.VMEM((M, 2 * HEAD_SIZE), jnp.bfloat16),
            pltpu.VMEM((HEAD_SIZE + ONES, M), jnp.float32),
            pltpu.VMEM((8, M), jnp.float32),
            pltpu.SemaphoreType.DMA((2, tiles)),
        ],
        compiler_params=pltpu.CompilerParams(vmem_limit_bytes=56 << 20),
        name="attend",
    )(info, q, k, v)


BLK_ULY = ("blk_0", "blk_1", "blk_2", "uly")
BLK = ("blk_0", "blk_1", "blk_2")


def local(queries, keys, values, segments):
    heads = lax.axis_size("uly")
    columns = lax.axis_size("blk_0")
    rows = queries.shape[0]
    piece = rows // columns
    width = queries.shape[1] // heads
    counts = jnp.sum((segments[None, :] < jnp.arange(NDOC, dtype=jnp.int32)[:, None]).astype(jnp.int32), axis=1)
    starts = lax.psum(counts, BLK_ULY)
    place = lax.axis_index(("blk_1", "blk_2")) * UNIT
    info = jnp.concatenate([starts, jnp.stack([place, lax.axis_index("blk_0") * piece]).astype(jnp.int32)])
    q = queries.reshape(columns, piece, heads, width)
    q = lax.all_to_all(q, "uly", split_axis=2, concat_axis=1, tiled=True)
    q = q.reshape(columns, heads, piece, width)
    q = lax.all_to_all(q, "blk_0", split_axis=0, concat_axis=0, tiled=True)
    kv = jnp.stack([keys, values])
    kv = lax.all_to_all(kv, "uly", split_axis=2, concat_axis=1, tiled=True)
    kv = lax.all_gather(kv, BLK, axis=1, tiled=True)
    out = attention(info, q, kv[0], kv[1])
    out = lax.all_to_all(out, "blk_0", split_axis=0, concat_axis=0, tiled=True)
    out = lax.all_to_all(out, "uly", split_axis=1, concat_axis=3, tiled=True)
    return out.reshape(rows, heads * width)


def solution(mesh):
    split = Mesh(mesh.devices.reshape(4, 4, 2, mesh.shape["uly"]), BLK_ULY)
    return jax.shard_map(
        local,
        mesh=split,
        in_specs=(P(BLK_ULY, None), P(BLK_ULY, None), P(BLK_ULY, None), P(BLK_ULY)),
        out_specs=P(BLK_ULY, None),
        check_vma=False,
    )
```

```python
import functools
import jax, jax.numpy as jnp
from jax import lax
from jax.experimental import pallas as pl
from jax.experimental.pallas import tpu as pltpu
from jax.sharding import Mesh
from jax.sharding import PartitionSpec as P

HEAD_SIZE = 128
NDOC = 8
GROUP = 8
SCALE2 = 1.4426950408889634 * HEAD_SIZE ** -0.5
ONES = 16
UNIT = 512
BIG = 2048


def doc_start(info, pos):
    low = jnp.zeros_like(pos)
    for d in range(1, NDOC):
        low = jnp.where(info[d, 0] <= pos, jnp.maximum(low, info[d, 0]), low)
    return low


def contract(a, b, da, db):
    return lax.dot_general(a, b, (((da,), (db,)), ((), ())), preferred_element_type=jnp.float32)


def attend(place, info, q_ref, kv, o_ref, kbuf, vbuf, qcat, acc, top, sems):
    D = HEAD_SIZE
    piece = q_ref.shape[1]
    tiles = pieces = RING
    rows = pieces * piece
    M = GROUP * rows
    blocks = kbuf.shape[0] // tiles
    part = blocks * UNIT
    offset, stripe = place()
    shard = UNIT // pieces

    def loads(t):
        at = pl.ds(t * blocks, blocks)
        return (
            pltpu.make_async_copy(kv.at[at, pl.ds(0, UNIT)], kbuf.at[at], sems.at[0, t]),
            pltpu.make_async_copy(kv.at[at, pl.ds(UNIT, UNIT)], vbuf.at[at], sems.at[1, t]),
        )

    for t in range(tiles):
        for c in loads(t):
            c.start()

    @pl.loop(0, tiles)
    def _(t):
        base = offset + t * part
        first = base + stripe
        last = first + (pieces - 1) * shard + piece - 1
        for c in loads(t):
            c.wait()
        low = doc_start(info, first) // UNIT
        diag = base // UNIT
        lane = lax.broadcasted_iota(jnp.int32, (1, rows), 1)
        qpos = first + (lane // piece) * shard + lane % piece
        qlow = doc_start(info, qpos)

        for g in range(GROUP):
            q = q_ref[pl.ds(t * pieces, pieces), :, g * D:(g + 1) * D].reshape(rows, D).astype(jnp.float32) * SCALE2
            high = q.astype(jnp.bfloat16)
            at = slice(g * rows, (g + 1) * rows)
            qcat[at, :D] = high
            qcat[at, D:] = (q - high.astype(jnp.float32)).astype(jnp.bfloat16)
        acc[...] = jnp.zeros_like(acc)

        def allowed(at, size):
            kpos = at + lax.broadcasted_iota(jnp.int32, (size, rows), 0)
            return (kpos <= qpos) & (kpos >= qlow)

        def masked(p, m):
            return jnp.concatenate(
                [jnp.where(m, p[:, g * rows:(g + 1) * rows], 0.0) for g in range(p.shape[1] // rows)], axis=1)

        def step(at, size):
            k = kbuf[pl.ds(at, size // UNIT)].reshape(size, D)
            v = vbuf[pl.ds(at, size // UNIT)].reshape(size, D)
            kk = jnp.concatenate([k, k], axis=1)
            vv = jnp.concatenate([v, jnp.ones((size, ONES), v.dtype)], axis=1)
            p = masked(jnp.exp2(contract(kk, qcat[...], 1, 1)), allowed(at * UNIT, size))
            acc[...] += contract(vv, p.astype(jnp.bfloat16), 0, 0)

        units = diag + 1 - low
        per = BIG // UNIT
        big = units // per

        @pl.loop(0, big)
        def _(n):
            step(low + n * per, BIG)

        size = BIG // 2
        done = low + big * per
        while size >= UNIT:
            some = (units // (size // UNIT)) % 2

            @pl.when(some == 1)
            def _(done=done, size=size):
                step(done, size)

            done = done + some * (size // UNIT)
            size //= 2

        total = acc[D:D + 8, :]
        good = jnp.min(jnp.where((total > 2.0 ** -60) & (total < 2.0 ** 118), 1.0, 0.0))

        @pl.when(good < 0.5)
        def _():
            top[...] = jnp.full_like(top, -1e30)
            acc[...] = jnp.zeros_like(acc)

            def scores(n, g):
                q = q_ref[pl.ds(t * pieces, pieces), :, pl.ds(pl.multiple_of(g * D, D), D)].reshape(rows, D)
                m = allowed(n * UNIT, UNIT)
                return jnp.where(m, contract(kbuf[n], q, 1, 1) * SCALE2, -1e30), m

            @pl.loop(low, diag + 1)
            def _(n):
                @pl.loop(0, GROUP)
                def _(g):
                    at = pl.ds(pl.multiple_of(g * rows, rows), rows)
                    s, _ = scores(n, g)
                    top[:, at] = jnp.maximum(top[:, at], jnp.max(s, axis=0, keepdims=True))

            @pl.loop(low, diag + 1)
            def _(n):
                v = vbuf[n]
                vv = jnp.concatenate([v, jnp.ones((UNIT, ONES), v.dtype)], axis=1)

                @pl.loop(0, GROUP)
                def _(g):
                    at = pl.ds(pl.multiple_of(g * rows, rows), rows)
                    s, m = scores(n, g)
                    p = jnp.where(m, jnp.exp2(s - top[:1, at]), 0.0)
                    acc[:, at] += contract(vv, p.astype(jnp.bfloat16), 0, 0)

        for g in range(GROUP):
            at = slice(g * rows, (g + 1) * rows)
            out = acc[:D, at] / acc[D:D + 1, at]
            o_ref[pl.ds(t * pieces, pieces), :, g * D:(g + 1) * D] = out.T.astype(jnp.bfloat16).reshape(pieces, piece, D)


def place():
    return (
        lax.axis_index(("blk_1", "blk_2")) * UNIT,
        lax.axis_index("blk_0") * (UNIT // RING // RING),
    )


def attention(starts, q, kv, place=place):
    M = GROUP * RING * q.shape[1]
    vm = pl.BlockSpec(memory_space=pltpu.VMEM)
    half = (kv.shape[0], UNIT, HEAD_SIZE)
    return pl.pallas_call(
        functools.partial(attend, place),
        out_shape=jax.ShapeDtypeStruct(q.shape, jnp.bfloat16),
        in_specs=[pl.BlockSpec(memory_space=pltpu.SMEM), vm, pl.BlockSpec(memory_space=pl.ANY)],
        out_specs=vm,
        scratch_shapes=[
            pltpu.VMEM(half, jnp.bfloat16),
            pltpu.VMEM(half, jnp.bfloat16),
            pltpu.VMEM((M, 2 * HEAD_SIZE), jnp.bfloat16),
            pltpu.VMEM((HEAD_SIZE + ONES, M), jnp.float32),
            pltpu.VMEM((8, M), jnp.float32),
            pltpu.SemaphoreType.DMA((2, RING)),
        ],
        compiler_params=pltpu.CompilerParams(vmem_limit_bytes=56 << 20),
        name="attend",
    )(starts, q, kv)


AXES = ("blk_0", "blk_1", "blk_2", "uly")
RING = 4
K_ROWS = UNIT
FIRST_ROWS = 768


def coordinates():
    return {axis: lax.axis_index(axis) for axis in AXES}


def shifted(at, axis, by):
    size = 2 if axis == "blk_2" else RING
    return lax.rem(at[axis] + (by + size), size)


def greet(peers):
    barrier = pltpu.get_barrier_semaphore()
    for peer in peers:
        pl.semaphore_signal(barrier, inc=1, device_id=peer, device_id_type=pl.DeviceIdType.MESH)
    pl.semaphore_wait(barrier, len(peers))


def remote(src, dst, send, recv, peer):
    return pltpu.make_async_remote_copy(
        src_ref=src, dst_ref=dst, send_sem=send, recv_sem=recv, device_id=peer,
        device_id_type=pl.DeviceIdType.MESH)


def square_peers(at):
    return [
        {"blk_0": shifted(at, "blk_0", i), "uly": shifted(at, "uly", j)}
        for i in range(RING) for j in range(RING) if i or j
    ]


def exchange(seg, q_in, k_in, v_in, q_out, kv, count_out, counts, own_sem, q_sem, z_sem, c_sem, stream_send, stream_recv, core_sem):
    D = HEAD_SIZE
    at = coordinates()
    x, y, c, z = (at[a] for a in AXES)
    rows = q_in.shape[0]
    piece = rows // RING
    width = q_in.shape[1] // RING
    greet(square_peers(at) + [{"blk_1": shifted(at, "blk_1", j)} for j in range(1, RING)] + [{"blk_2": 1 - c}])

    def block(i, j):
        return (shifted(at, "blk_0", i) * RING + shifted(at, "blk_1", j)) * 2 + c

    me = block(0, 0)
    mine = pl.ds(pl.multiple_of(z * rows, rows), rows)
    low = pl.ds(pl.multiple_of(UNIT + z * rows, rows), rows)

    def head(ref, h):
        return ref.at[:, pl.ds(pl.multiple_of(h * D, D), D)]

    own = [
        pltpu.make_async_copy(head(k_in, z), kv.at[me, mine], own_sem.at[0]),
        pltpu.make_async_copy(head(v_in, z), kv.at[me, low], own_sem.at[1]),
    ]
    for copy in own:
        copy.start()
    for j in range(1, RING):
        to = shifted(at, "uly", j)
        remote(head(k_in, to), kv.at[me, mine], z_sem.at[0], z_sem.at[1], {"uly": to}).start()
        remote(head(v_in, to), kv.at[me, low], z_sem.at[0], z_sem.at[1], {"uly": to}).start()

    def q_part(i, j):
        return q_in.at[pl.ds(pl.multiple_of(i * piece, piece), piece), pl.ds(pl.multiple_of(j * width, width), width)]

    q_own = pltpu.make_async_copy(q_part(x, z), q_out.at[x * RING + z], own_sem.at[2])
    q_own.start()

    def send_counts(phase, axis, value):
        size = 2 if axis == "blk_2" else RING
        counts[phase, 0] = value
        for j in range(1, size):
            remote(counts.at[phase, 0], counts.at[phase, size - j], c_sem.at[0, phase], c_sem.at[1, phase],
                   {axis: shifted(at, axis, j)}).start()

    def sum_counts(phase, axis):
        size = 2 if axis == "blk_2" else RING
        got = counts.at[phase, pl.ds(1, size - 1)]
        remote(got, got, c_sem.at[0, phase], c_sem.at[1, phase], {axis: shifted(at, axis, 1)}).wait()
        total = counts[phase, 0]
        for j in range(1, size):
            total = total + counts[phase, j]
        return total

    docs = lax.broadcasted_iota(jnp.int32, (NDOC, seg.shape[1]), 0)
    send_counts(0, "uly", jnp.where(seg[...] < docs, 1, 0))

    for peer in square_peers(at):
        i, j = (peer["blk_0"], peer["uly"])
        remote(q_part(i, j), q_out.at[x * RING + z], q_sem.at[0], q_sem.at[1], peer).start()

    for copy in own:
        copy.wait()
    got = kv.at[0, pl.ds(0, 2 * (RING - 1) * rows)]
    remote(got, got, z_sem.at[0], z_sem.at[1], {"uly": shifted(at, "uly", 1)}).wait()

    streams = (
        (0, 0, FIRST_ROWS, "blk_0", "blk_1"),
        (1, FIRST_ROWS, 2 * UNIT - FIRST_ROWS, "blk_1", "blk_0"),
    )
    order = (0, -1, 1, 2)

    def region(stream, i, j, half=None):
        _, start, size, first, _ = stream
        if half is not None:
            size //= 2
            start += half * size
        return kv.at[block(i, j) if first == "blk_0" else block(j, i), pl.ds(start, size)]

    def ring_copy(stream, what, axis, by, slot):
        return remote(what, what, stream_send.at[stream[0]], stream_recv.at[stream[0], slot], {axis: shifted(at, axis, by)})

    def to_core(what):
        remote(what, what, core_sem.at[0], core_sem.at[1], {"blk_2": 1 - c}).start()

    def spread(stream, axis, slot, pick):
        ring_copy(stream, pick(0), axis, 1, slot).start()
        ring_copy(stream, pick(0), axis, -1, slot + 1).start()

    def relay(stream, axis, slot, pick):
        ring_copy(stream, pick(-1), axis, 1, slot).wait_recv()
        ring_copy(stream, pick(-1, 0), axis, 1, slot + 2).start()
        ring_copy(stream, pick(1), axis, -1, slot + 1).wait_recv()
        ring_copy(stream, pick(1, 1), axis, -1, slot + 3).start()

    def settle(stream, axis, slot, pick):
        ring_copy(stream, pick(2, 0), axis, 1, slot + 2).wait_recv()
        ring_copy(stream, pick(2, 1), axis, -1, slot + 3).wait_recv()

    def along_first(stream):
        return lambda i, half=None: region(stream, i, 0, half)

    def along_second(stream, i):
        return lambda j, half=None: region(stream, i, j, half)

    for s in streams:
        spread(s, s[3], 0, along_first(s))
    for s in streams:
        spread(s, s[4], 4, along_second(s, 0))
    to_core(kv.at[me])
    send_counts(1, "blk_0", sum_counts(0, "uly"))
    for s in streams:
        relay(s, s[3], 0, along_first(s))
        for n in (1, 2):
            spread(s, s[4], 4 + 4 * n, along_second(s, order[n]))
            to_core(region(s, order[n], 0))
    send_counts(2, "blk_1", sum_counts(1, "blk_0"))
    for s in streams:
        relay(s, s[4], 4, along_second(s, 0))
        to_core(region(s, 0, -1))
        to_core(region(s, 0, 1))
    for s in streams:
        settle(s, s[3], 0, along_first(s))
        spread(s, s[4], 16, along_second(s, 2))
        to_core(region(s, 2, 0))
    send_counts(3, "blk_2", sum_counts(2, "blk_1"))
    for n in (1, 2, 3):
        for s in streams:
            settle(s, s[4], 4 * n, along_second(s, order[n - 1]))
            to_core(region(s, order[n - 1], 2))
            relay(s, s[4], 4 + 4 * n, along_second(s, order[n]))
            to_core(region(s, order[n], -1))
            to_core(region(s, order[n], 1))
    count_out[...] = jnp.broadcast_to(jnp.sum(sum_counts(3, "blk_2"), axis=1, keepdims=True), count_out.shape)
    for s in streams:
        settle(s, s[4], 16, along_second(s, 2))
        to_core(region(s, 2, 2))
    for s in streams:
        sent = kv.at[pl.ds(0, 15), pl.ds(s[1], s[2])]
        ring_copy(s, sent, s[3], 1, 0).wait_send()
    half = kv.at[pl.ds(0, 16)]
    remote(half, half, core_sem.at[0], core_sem.at[1], {"blk_2": 1 - c}).wait()
    q_own.wait()
    most = q_out.at[pl.ds(0, RING * RING - 1)]
    remote(most, most, q_sem.at[0], q_sem.at[1], {"uly": shifted(at, "uly", 1)}).wait()


def give_back(o_in, out, own_sem, sem):
    at = coordinates()
    x, z = at["blk_0"], at["uly"]
    piece, width = o_in.shape[1:]
    peers = square_peers(at)
    greet(peers)
    here = out.at[pl.ds(pl.multiple_of(x * piece, piece), piece), pl.ds(pl.multiple_of(z * width, width), width)]
    own = pltpu.make_async_copy(o_in.at[x * RING + z], here, own_sem)
    for peer in peers:
        remote(o_in.at[peer["blk_0"] * RING + peer["uly"]], here, sem.at[0], sem.at[1], peer).start()
    own.start()
    own.wait()
    most = o_in.at[pl.ds(0, RING * RING - 1)]
    remote(most, most, sem.at[0], sem.at[1], peers[0]).wait()


def local(queries, keys, values, segments):
    rows, wide = queries.shape
    piece, width = rows // RING, wide // RING
    anywhere = pl.BlockSpec(memory_space=pl.ANY)
    vm = pl.BlockSpec(memory_space=pltpu.VMEM)
    q, kv, starts = pl.pallas_call(
        exchange,
        out_shape=(
            jax.ShapeDtypeStruct((RING * RING, piece, width), jnp.bfloat16),
            jax.ShapeDtypeStruct((2 * RING * RING, 2 * UNIT, HEAD_SIZE), jnp.bfloat16),
            jax.ShapeDtypeStruct((NDOC, 128), jnp.int32),
        ),
        in_specs=[vm, anywhere, anywhere, anywhere],
        out_specs=(anywhere, anywhere, vm),
        scratch_shapes=[
            pltpu.VMEM((4, RING, NDOC, rows), jnp.int32),
            pltpu.SemaphoreType.DMA((3,)),
            pltpu.SemaphoreType.DMA((2,)),
            pltpu.SemaphoreType.DMA((2,)),
            pltpu.SemaphoreType.DMA((2, 4)),
            pltpu.SemaphoreType.DMA((2,)),
            pltpu.SemaphoreType.DMA((2, 20)),
            pltpu.SemaphoreType.DMA((2,)),
        ],
        compiler_params=pltpu.CompilerParams(collective_id=0, has_side_effects=True),
        name="exchange",
    )(segments.reshape(1, rows), queries, keys, values)
    out = attention(starts, q, kv)
    return pl.pallas_call(
        give_back,
        out_shape=jax.ShapeDtypeStruct((rows, wide), jnp.bfloat16),
        in_specs=[anywhere],
        out_specs=anywhere,
        scratch_shapes=[pltpu.SemaphoreType.DMA, pltpu.SemaphoreType.DMA((2,))],
        compiler_params=pltpu.CompilerParams(collective_id=1, has_side_effects=True),
        name="give_back",
    )(out)


def solution(mesh):
    split = Mesh(mesh.devices.reshape(4, 4, 2, mesh.shape["uly"]), AXES)
    return jax.shard_map(
        local,
        mesh=split,
        in_specs=(P(AXES, None), P(AXES, None), P(AXES, None), P(AXES)),
        out_specs=P(AXES, None),
        check_vma=False,
    )
```

```python
import functools
import jax, jax.numpy as jnp
from jax import lax
from jax.experimental import pallas as pl
from jax.experimental.pallas import tpu as pltpu
from jax.sharding import Mesh
from jax.sharding import PartitionSpec as P

HEAD_SIZE = 128
NDOC = 8
GROUP = 8
SCALE2 = 1.4426950408889634 * HEAD_SIZE ** -0.5
ONES = 16
UNIT = 512
BIG = 2048


def doc_start(info, pos):
    low = jnp.zeros_like(pos)
    for d in range(1, NDOC):
        low = jnp.where(info[d, 0] <= pos, jnp.maximum(low, info[d, 0]), low)
    return low


def contract(a, b, da, db):
    return lax.dot_general(a, b, (((da,), (db,)), ((), ())), preferred_element_type=jnp.float32)


def attend(place, info, q_ref, kv, o_ref, kbuf, vbuf, qcat, acc, top, sems):
    D = HEAD_SIZE
    piece = q_ref.shape[1]
    tiles = pieces = RING
    rows = pieces * piece
    M = GROUP * rows
    blocks = kbuf.shape[0] // tiles
    part = blocks * UNIT
    offset, stripe = place()
    shard = UNIT // pieces

    def loads(t):
        at = pl.ds(t * blocks, blocks)
        return (
            pltpu.make_async_copy(kv.at[at, pl.ds(0, UNIT)], kbuf.at[at], sems.at[0, t]),
            pltpu.make_async_copy(kv.at[at, pl.ds(UNIT, UNIT)], vbuf.at[at], sems.at[1, t]),
        )

    for t in range(tiles):
        for c in loads(t):
            c.start()

    @pl.loop(0, tiles)
    def _(t):
        base = offset + t * part
        first = base + stripe
        last = first + (pieces - 1) * shard + piece - 1
        for c in loads(t):
            c.wait()
        low = doc_start(info, first) // UNIT
        diag = base // UNIT
        lane = lax.broadcasted_iota(jnp.int32, (1, rows), 1)
        qpos = first + (lane // piece) * shard + lane % piece
        qlow = doc_start(info, qpos)

        for g in range(GROUP):
            q = q_ref[pl.ds(t * pieces, pieces), :, g * D:(g + 1) * D].reshape(rows, D).astype(jnp.float32) * SCALE2
            high = q.astype(jnp.bfloat16)
            at = slice(g * rows, (g + 1) * rows)
            qcat[at, :D] = high
            qcat[at, D:] = (q - high.astype(jnp.float32)).astype(jnp.bfloat16)
        acc[...] = jnp.zeros_like(acc)

        def allowed(at, size):
            kpos = at + lax.broadcasted_iota(jnp.int32, (size, rows), 0)
            return (kpos <= qpos) & (kpos >= qlow)

        def masked(p, m):
            return jnp.concatenate(
                [jnp.where(m, p[:, g * rows:(g + 1) * rows], 0.0) for g in range(p.shape[1] // rows)], axis=1)

        def step(at, size):
            k = kbuf[pl.ds(at, size // UNIT)].reshape(size, D)
            v = vbuf[pl.ds(at, size // UNIT)].reshape(size, D)
            kk = jnp.concatenate([k, k], axis=1)
            vv = jnp.concatenate([v, jnp.ones((size, ONES), v.dtype)], axis=1)
            p = masked(jnp.exp2(contract(kk, qcat[...], 1, 1)), allowed(at * UNIT, size))
            acc[...] += contract(vv, p.astype(jnp.bfloat16), 0, 0)

        units = diag + 1 - low
        per = BIG // UNIT
        big = units // per

        @pl.loop(0, big)
        def _(n):
            step(low + n * per, BIG)

        size = BIG // 2
        done = low + big * per
        while size >= UNIT:
            some = (units // (size // UNIT)) % 2

            @pl.when(some == 1)
            def _(done=done, size=size):
                step(done, size)

            done = done + some * (size // UNIT)
            size //= 2

        total = acc[D:D + 8, :]
        good = jnp.min(jnp.where((total > 2.0 ** -60) & (total < 2.0 ** 118), 1.0, 0.0))

        @pl.when(good < 0.5)
        def _():
            top[...] = jnp.full_like(top, -1e30)
            acc[...] = jnp.zeros_like(acc)

            def scores(n, g):
                q = q_ref[pl.ds(t * pieces, pieces), :, pl.ds(pl.multiple_of(g * D, D), D)].reshape(rows, D)
                m = allowed(n * UNIT, UNIT)
                return jnp.where(m, contract(kbuf[n], q, 1, 1) * SCALE2, -1e30), m

            @pl.loop(low, diag + 1)
            def _(n):
                @pl.loop(0, GROUP)
                def _(g):
                    at = pl.ds(pl.multiple_of(g * rows, rows), rows)
                    s, _ = scores(n, g)
                    top[:, at] = jnp.maximum(top[:, at], jnp.max(s, axis=0, keepdims=True))

            @pl.loop(low, diag + 1)
            def _(n):
                v = vbuf[n]
                vv = jnp.concatenate([v, jnp.ones((UNIT, ONES), v.dtype)], axis=1)

                @pl.loop(0, GROUP)
                def _(g):
                    at = pl.ds(pl.multiple_of(g * rows, rows), rows)
                    s, m = scores(n, g)
                    p = jnp.where(m, jnp.exp2(s - top[:1, at]), 0.0)
                    acc[:, at] += contract(vv, p.astype(jnp.bfloat16), 0, 0)

        for g in range(GROUP):
            at = slice(g * rows, (g + 1) * rows)
            out = acc[:D, at] / acc[D:D + 1, at]
            o_ref[pl.ds(t * pieces, pieces), :, g * D:(g + 1) * D] = out.T.astype(jnp.bfloat16).reshape(pieces, piece, D)


def place():
    return (
        lax.axis_index(("blk_1", "blk_2")) * UNIT,
        lax.axis_index("blk_0") * (UNIT // RING // RING),
    )


def attention(starts, q, kv, place=place):
    M = GROUP * RING * q.shape[1]
    vm = pl.BlockSpec(memory_space=pltpu.VMEM)
    half = (kv.shape[0], UNIT, HEAD_SIZE)
    return pl.pallas_call(
        functools.partial(attend, place),
        out_shape=jax.ShapeDtypeStruct(q.shape, jnp.bfloat16),
        in_specs=[pl.BlockSpec(memory_space=pltpu.SMEM), vm, pl.BlockSpec(memory_space=pl.ANY)],
        out_specs=vm,
        scratch_shapes=[
            pltpu.VMEM(half, jnp.bfloat16),
            pltpu.VMEM(half, jnp.bfloat16),
            pltpu.VMEM((M, 2 * HEAD_SIZE), jnp.bfloat16),
            pltpu.VMEM((HEAD_SIZE + ONES, M), jnp.float32),
            pltpu.VMEM((8, M), jnp.float32),
            pltpu.SemaphoreType.DMA((2, RING)),
        ],
        compiler_params=pltpu.CompilerParams(vmem_limit_bytes=56 << 20),
        name="attend",
    )(starts, q, kv)


AXES = ("blk_0", "blk_1", "blk_2", "uly")
RING = 4
K_ROWS = UNIT
FIRST_ROWS = 768


def coordinates():
    return {axis: lax.axis_index(axis) for axis in AXES}


def shifted(at, axis, by):
    size = 2 if axis == "blk_2" else RING
    return lax.rem(at[axis] + (by + size), size)


def greet(peers):
    barrier = pltpu.get_barrier_semaphore()
    for peer in peers:
        pl.semaphore_signal(barrier, inc=1, device_id=peer, device_id_type=pl.DeviceIdType.MESH)
    pl.semaphore_wait(barrier, len(peers))


def remote(src, dst, send, recv, peer):
    return pltpu.make_async_remote_copy(
        src_ref=src, dst_ref=dst, send_sem=send, recv_sem=recv, device_id=peer,
        device_id_type=pl.DeviceIdType.MESH)


def square_peers(at):
    return [
        {"blk_0": shifted(at, "blk_0", i), "uly": shifted(at, "uly", j)}
        for i in range(RING) for j in range(RING) if i or j
    ]


def exchange(seg, q_in, k_in, v_in, q_out, kv, count_out, counts, own_sem, q_sem, z_sem, c_sem, stream_send, stream_recv, core_sem):
    D = HEAD_SIZE
    at = coordinates()
    x, y, c, z = (at[a] for a in AXES)
    rows = q_in.shape[0]
    piece = rows // RING
    width = q_in.shape[1] // RING
    greet(square_peers(at) + [{"blk_1": shifted(at, "blk_1", j)} for j in range(1, RING)] + [{"blk_2": 1 - c}])

    def block(i, j):
        return (shifted(at, "blk_0", i) * RING + shifted(at, "blk_1", j)) * 2 + c

    me = block(0, 0)
    mine = pl.ds(pl.multiple_of(z * rows, rows), rows)
    low = pl.ds(pl.multiple_of(UNIT + z * rows, rows), rows)

    def head(ref, h):
        return ref.at[:, pl.ds(pl.multiple_of(h * D, D), D)]

    own = [
        pltpu.make_async_copy(head(k_in, z), kv.at[me, mine], own_sem.at[0]),
        pltpu.make_async_copy(head(v_in, z), kv.at[me, low], own_sem.at[1]),
    ]
    for copy in own:
        copy.start()
    for j in range(1, RING):
        to = shifted(at, "uly", j)
        remote(head(k_in, to), kv.at[me, mine], z_sem.at[0], z_sem.at[1], {"uly": to}).start()
        remote(head(v_in, to), kv.at[me, low], z_sem.at[0], z_sem.at[1], {"uly": to}).start()

    def q_part(i, j):
        return q_in.at[pl.ds(pl.multiple_of(i * piece, piece), piece), pl.ds(pl.multiple_of(j * width, width), width)]

    q_own = pltpu.make_async_copy(q_part(x, z), q_out.at[x * RING + z], own_sem.at[2])
    q_own.start()

    def send_counts(phase, axis, value):
        size = 2 if axis == "blk_2" else RING
        counts[phase, 0] = value
        for j in range(1, size):
            remote(counts.at[phase, 0], counts.at[phase, size - j], c_sem.at[0, phase], c_sem.at[1, phase],
                   {axis: shifted(at, axis, j)}).start()

    def sum_counts(phase, axis):
        size = 2 if axis == "blk_2" else RING
        got = counts.at[phase, pl.ds(1, size - 1)]
        remote(got, got, c_sem.at[0, phase], c_sem.at[1, phase], {axis: shifted(at, axis, 1)}).wait()
        total = counts[phase, 0]
        for j in range(1, size):
            total = total + counts[phase, j]
        return total

    docs = lax.broadcasted_iota(jnp.int32, (NDOC, seg.shape[1]), 0)
    send_counts(0, "uly", jnp.where(seg[...] < docs, 1, 0))

    for peer in square_peers(at):
        i, j = (peer["blk_0"], peer["uly"])
        remote(q_part(i, j), q_out.at[x * RING + z], q_sem.at[0], q_sem.at[1], peer).start()

    for copy in own:
        copy.wait()
    got = kv.at[0, pl.ds(0, 2 * (RING - 1) * rows)]
    remote(got, got, z_sem.at[0], z_sem.at[1], {"uly": shifted(at, "uly", 1)}).wait()

    streams = (
        (0, 0, FIRST_ROWS, "blk_0", "blk_1"),
        (1, FIRST_ROWS, 2 * UNIT - FIRST_ROWS, "blk_1", "blk_0"),
    )
    order = (0, -1, 1, 2)

    def region(stream, i, j, half=None):
        _, start, size, first, _ = stream
        if half is not None:
            size //= 2
            start += half * size
        return kv.at[block(i, j) if first == "blk_0" else block(j, i), pl.ds(start, size)]

    def ring_copy(stream, what, axis, by, slot):
        return remote(what, what, stream_send.at[stream[0]], stream_recv.at[stream[0], slot], {axis: shifted(at, axis, by)})

    def to_core(what):
        remote(what, what, core_sem.at[0], core_sem.at[1], {"blk_2": 1 - c}).start()

    def spread(stream, axis, slot, pick):
        ring_copy(stream, pick(0), axis, 1, slot).start()
        ring_copy(stream, pick(0), axis, -1, slot + 1).start()

    def relay(stream, axis, slot, pick):
        ring_copy(stream, pick(-1), axis, 1, slot).wait_recv()
        ring_copy(stream, pick(-1, 0), axis, 1, slot + 2).start()
        ring_copy(stream, pick(1), axis, -1, slot + 1).wait_recv()
        ring_copy(stream, pick(1, 1), axis, -1, slot + 3).start()

    def settle(stream, axis, slot, pick):
        ring_copy(stream, pick(2, 0), axis, 1, slot + 2).wait_recv()
        ring_copy(stream, pick(2, 1), axis, -1, slot + 3).wait_recv()

    def along_first(stream):
        return lambda i, half=None: region(stream, i, 0, half)

    def along_second(stream, i):
        return lambda j, half=None: region(stream, i, j, half)

    for s in streams:
        spread(s, s[3], 0, along_first(s))
    for s in streams:
        spread(s, s[4], 4, along_second(s, 0))
    to_core(kv.at[me])
    send_counts(1, "blk_0", sum_counts(0, "uly"))
    for s in streams:
        relay(s, s[3], 0, along_first(s))
        for n in (1, 2):
            spread(s, s[4], 4 + 4 * n, along_second(s, order[n]))
            to_core(region(s, order[n], 0))
    send_counts(2, "blk_1", sum_counts(1, "blk_0"))
    for s in streams:
        relay(s, s[4], 4, along_second(s, 0))
        to_core(region(s, 0, -1))
        to_core(region(s, 0, 1))
    for s in streams:
        settle(s, s[3], 0, along_first(s))
        spread(s, s[4], 16, along_second(s, 2))
        to_core(region(s, 2, 0))
    send_counts(3, "blk_2", sum_counts(2, "blk_1"))
    for n in (1, 2, 3):
        for s in streams:
            settle(s, s[4], 4 * n, along_second(s, order[n - 1]))
            to_core(region(s, order[n - 1], 2))
            relay(s, s[4], 4 + 4 * n, along_second(s, order[n]))
            to_core(region(s, order[n], -1))
            to_core(region(s, order[n], 1))
    count_out[...] = jnp.broadcast_to(jnp.sum(sum_counts(3, "blk_2"), axis=1, keepdims=True), count_out.shape)
    for s in streams:
        settle(s, s[4], 16, along_second(s, 2))
        to_core(region(s, 2, 2))
    for s in streams:
        sent = kv.at[pl.ds(0, 15), pl.ds(s[1], s[2])]
        ring_copy(s, sent, s[3], 1, 0).wait_send()
    half = kv.at[pl.ds(0, 16)]
    remote(half, half, core_sem.at[0], core_sem.at[1], {"blk_2": 1 - c}).wait()
    q_own.wait()
    most = q_out.at[pl.ds(0, RING * RING - 1)]
    remote(most, most, q_sem.at[0], q_sem.at[1], {"uly": shifted(at, "uly", 1)}).wait()


def give_back(o_in, out, own_sem, sem):
    at = coordinates()
    x, z = at["blk_0"], at["uly"]
    piece, width = o_in.shape[1:]
    peers = square_peers(at)
    greet(peers)
    here = out.at[pl.ds(pl.multiple_of(x * piece, piece), piece), pl.ds(pl.multiple_of(z * width, width), width)]
    own = pltpu.make_async_copy(o_in.at[x * RING + z], here, own_sem)
    for peer in peers:
        remote(o_in.at[peer["blk_0"] * RING + peer["uly"]], here, sem.at[0], sem.at[1], peer).start()
    own.start()
    own.wait()
    most = o_in.at[pl.ds(0, RING * RING - 1)]
    remote(most, most, sem.at[0], sem.at[1], peers[0]).wait()


def careful(queries, keys, values, segments):
    rows, wide = queries.shape
    piece, width = rows // RING, wide // RING
    anywhere = pl.BlockSpec(memory_space=pl.ANY)
    vm = pl.BlockSpec(memory_space=pltpu.VMEM)
    q, kv, starts = pl.pallas_call(
        exchange,
        out_shape=(
            jax.ShapeDtypeStruct((RING * RING, piece, width), jnp.bfloat16),
            jax.ShapeDtypeStruct((2 * RING * RING, 2 * UNIT, HEAD_SIZE), jnp.bfloat16),
            jax.ShapeDtypeStruct((NDOC, 128), jnp.int32),
        ),
        in_specs=[vm, anywhere, anywhere, anywhere],
        out_specs=(anywhere, anywhere, vm),
        scratch_shapes=[
            pltpu.VMEM((4, RING, NDOC, rows), jnp.int32),
            pltpu.SemaphoreType.DMA((3,)),
            pltpu.SemaphoreType.DMA((2,)),
            pltpu.SemaphoreType.DMA((2,)),
            pltpu.SemaphoreType.DMA((2, 4)),
            pltpu.SemaphoreType.DMA((2,)),
            pltpu.SemaphoreType.DMA((2, 20)),
            pltpu.SemaphoreType.DMA((2,)),
        ],
        compiler_params=pltpu.CompilerParams(collective_id=1, has_side_effects=True),
        name="exchange",
    )(segments.reshape(1, rows), queries, keys, values)
    out = attention(starts, q, kv)
    return pl.pallas_call(
        give_back,
        out_shape=jax.ShapeDtypeStruct((rows, wide), jnp.bfloat16),
        in_specs=[anywhere],
        out_specs=anywhere,
        scratch_shapes=[pltpu.SemaphoreType.DMA, pltpu.SemaphoreType.DMA((2,))],
        compiler_params=pltpu.CompilerParams(collective_id=2, has_side_effects=True),
        name="give_back",
    )(out)


COLUMN = 2 * UNIT
REACH = 8
CHUNK = 2080
CHUNKS = 4
WAITS = (
    (0, (1, 2), (0, 1, 2)),
    (1, (8,), ()),
    (2, (3,), ()),
    (4, (), (3, 4)),
    (6, (5, 6), ()),
    (7, (7,), ()),
    (8, (), (5, 6)),
    (9, (), (7, 8)),
)
LIMIT = 100.0


def ring_attend(seg, q_in, k_in, v_in, out, stats_out, kv, qbuf, obuf, qv, kv_own, qcat, acc, stats,
                local_sem, bar_z, q_sem, s_sem, send_sem, recv_sem, core_send, core_recv, o_sem):
    D = HEAD_SIZE
    x, y, c, z = (lax.axis_index(a) for a in AXES)
    column = x * RING + y
    rows = q_in.shape[0]
    width = q_in.shape[1] // RING

    def peer(axis, by):
        size = 2 if axis == "blk_2" else RING
        return {axis: lax.rem(lax.axis_index(axis) + by, size)}

    barrier = pltpu.get_barrier_semaphore()
    for axis in AXES:
        for by in range(1, 2 if axis == "blk_2" else RING):
            pl.semaphore_signal(barrier, inc=1, device_id=peer(axis, by), device_id_type=pl.DeviceIdType.MESH)
    pl.semaphore_wait(barrier, 10)

    def place(d, core):
        return pl.ds(pl.multiple_of((REACH - d) * COLUMN + core * UNIT, UNIT), UNIT)

    mine = pl.ds(pl.multiple_of(REACH * COLUMN + c * UNIT + z * rows, rows), rows)

    def head(ref, h, size):
        return ref.at[:, pl.ds(pl.multiple_of(h * size, size), size)]

    for j in (1, 3, 2):
        to = peer("uly", j)
        remote(head(k_in, to["uly"], D), kv.at[0, mine], bar_z.at[0], bar_z.at[1], to).start()
        remote(head(v_in, to["uly"], D), kv.at[1, mine], bar_z.at[0], bar_z.at[1], to).start()
    own = [
        pltpu.make_async_copy(head(k_in, z, D), kv.at[0, mine], local_sem.at[0]),
        pltpu.make_async_copy(head(v_in, z, D), kv.at[1, mine], local_sem.at[1]),
        pltpu.make_async_copy(head(q_in, z, width), qbuf.at[0], local_sem.at[2]),
        pltpu.make_async_copy(q_in, qv, local_sem.at[3]),
        pltpu.make_async_copy(k_in, kv_own, local_sem.at[4]),
    ]
    for copy in own:
        copy.start()
    for j in (1, 3, 2):
        to = peer("uly", j)
        remote(head(q_in, to["uly"], width), qbuf.at[RING - j], q_sem.at[0, j], q_sem.at[1, RING - j], to).start()

    @pl.loop(1, REACH + 1)
    def _(d):
        @pl.when(column < d)
        def _():
            at = pl.ds(pl.multiple_of((REACH - d) * COLUMN, COLUMN), COLUMN)
            kv[0, at] = jnp.zeros((COLUMN, D), kv.dtype)
            kv[1, at] = jnp.zeros((COLUMN, D), kv.dtype)

    own[3].wait()
    own[4].wait()

    def longest(ref):
        most = jnp.zeros((rows, 1), jnp.float32)
        for h in range(ref.shape[1] // D):
            a = ref[:, h * D:(h + 1) * D].astype(jnp.float32)
            most = jnp.maximum(most, jnp.sum(a * a, axis=1, keepdims=True))
        return jnp.broadcast_to(jnp.max(most, axis=0, keepdims=True), (1, rows))

    kind = lax.broadcasted_iota(jnp.int32, (2 * NDOC, rows), 0)
    before = jnp.where(seg[...] < kind, 1.0, 0.0)
    before = jnp.where(kind == NDOC, longest(qv), jnp.where(kind > NDOC, longest(kv_own), before))

    def send_stats(phase, axis, value):
        size = 2 if axis == "blk_2" else RING
        stats[phase, 0] = value
        for j in range(1, size):
            remote(stats.at[phase, 0], stats.at[phase, size - j], s_sem.at[0, phase], s_sem.at[1, phase], peer(axis, j)).start()

    def sum_stats(phase, axis):
        size = 2 if axis == "blk_2" else RING
        got = stats.at[phase, pl.ds(1, size - 1)]
        remote(got, got, s_sem.at[0, phase], s_sem.at[1, phase], peer(axis, 1)).wait()
        total = stats[phase, 0]
        for j in range(1, size):
            other = stats[phase, j]
            total = jnp.where(kind < NDOC, total + other, jnp.maximum(total, other))
        return total

    send_stats(0, "uly", before)
    own[0].wait()
    own[1].wait()
    got = kv.at[0, pl.ds(0, 2 * (RING - 1) * rows)]
    remote(got, got, bar_z.at[0], bar_z.at[1], peer("uly", 1)).wait()

    def move(n, from_d, to_d, to):
        return remote(kv.at[:, place(from_d, c)], kv.at[:, place(to_d, c)], send_sem.at[n], recv_sem.at[to_d], to)

    moves = []

    def start_if(able, *what):
        moves.append((able, what))

        @pl.when(able)
        def _():
            move(*what).start()

    def received(d):
        @pl.when(column >= d)
        def _():
            move(0, d, d, {"blk_1": y}).wait_recv()
            to_core(d).start()

    def to_core(d):
        what = kv.at[:, place(d, c)]
        return remote(what, what, core_send.at[d], core_recv.at[d], {"blk_2": 1 - c})

    def from_core(d):
        @pl.when(column >= d)
        def _():
            to_core(d).wait_recv()

    start_if(x < 3, 0, 0, 4, peer("blk_0", 1))
    start_if(x < 2, 1, 0, 8, peer("blk_0", 2))
    for j in (1, 3, 2):
        start_if(y + j < RING, 1 + j, 0, j, peer("blk_1", j))
    to_core(0).start()
    send_stats(1, "blk_0", sum_stats(0, "uly"))
    received(4)
    for j in (1, 3, 2):
        to = peer("blk_1", j)
        start_if(x >= 1, 4 + j, 4, 4 + to["blk_1"] - y, to)
    send_stats(2, "blk_1", sum_stats(1, "blk_0"))

    far = [((x >= 2) & (y >= j), (7 + j, 8, 8 - j, peer("blk_1", RING - j))) for j in (1, 3, 2)]
    moves.extend(far)

    def relay_far():
        for able, what in far:
            @pl.when(able)
            def _(what=what):
                move(*what).start()

    send_stats(3, "blk_2", sum_stats(2, "blk_1"))
    final = sum_stats(3, "blk_2")
    reach = final[NDOC:NDOC + 1] * final[NDOC + 1:NDOC + 2] * SCALE2 ** 2
    stats_out[...] = jnp.broadcast_to(jnp.where(reach < LIMIT ** 2, 1, 0), stats_out.shape)
    starts = jnp.sum(final[:NDOC], axis=1, keepdims=True).astype(jnp.int32)
    starts = jnp.broadcast_to(starts, (NDOC, rows))
    own[2].wait()

    @pl.loop(0, RING * CHUNKS)
    def _(n):
        early = n < 2 * RING
        turn = jnp.where(early, n % RING, (n - 2 * RING) // 2)
        chunk = jnp.where(early, n // RING, 2 + n % 2)
        to = lax.rem(z + turn, RING)

        for at_step, arrivals, crossed in WAITS:
            @pl.when(n == at_step)
            def _(arrivals=arrivals, crossed=crossed):
                for d in arrivals:
                    received(d)
                    if d == REACH:
                        relay_far()
                for d in crossed:
                    from_core(d)

        @pl.when(chunk == 0)
        def _():
            @pl.when(turn > 0)
            def _():
                remote(qbuf.at[turn], qbuf.at[turn], q_sem.at[0, turn], q_sem.at[1, turn], {"uly": to}).wait_recv()

            for g in range(GROUP):
                q = qbuf[turn, :, g * D:(g + 1) * D].astype(jnp.float32) * SCALE2
                high = q.astype(jnp.bfloat16)
                at = slice(g * rows, (g + 1) * rows)
                qcat[turn, at, :D] = high
                qcat[turn, at, D:] = (q - high.astype(jnp.float32)).astype(jnp.bfloat16)
            acc[turn] = jnp.zeros(acc.shape[1:], acc.dtype)

        qpos = column * COLUMN + c * UNIT + to * rows + lax.broadcasted_iota(jnp.int32, (1, rows), 1)
        qlow = jnp.zeros_like(qpos)
        for d in range(1, NDOC):
            qlow = jnp.where(starts[d:d + 1] <= qpos, jnp.maximum(qlow, starts[d:d + 1]), qlow)
        first = c * UNIT + to * rows + (CHUNKS - 1 - chunk) * CHUNK
        at = pl.ds(pl.multiple_of(first, 32), CHUNK)
        kpos = (column - REACH) * COLUMN + first + lax.broadcasted_iota(jnp.int32, (CHUNK, rows), 0)
        allowed = (kpos <= qpos) & (kpos >= qlow)
        k = kv[0, at]
        v = kv[1, at]
        kk = jnp.concatenate([k, k], axis=1)
        vv = jnp.concatenate([v, jnp.ones((CHUNK, ONES), v.dtype)], axis=1)
        p = jnp.exp2(contract(kk, qcat[turn], 1, 1))
        p = jnp.concatenate([jnp.where(allowed, p[:, g * rows:(g + 1) * rows], 0.0) for g in range(GROUP)], axis=1)
        acc[turn] += contract(vv, p.astype(jnp.bfloat16), 0, 0)

        @pl.when(chunk == CHUNKS - 1)
        def _():
            for g in range(GROUP):
                a = slice(g * rows, (g + 1) * rows)
                o = acc[turn, :D, a] / acc[turn, D:D + 1, a]
                obuf[turn, :, g * D:(g + 1) * D] = o.T.astype(jnp.bfloat16)

            @pl.when(turn == 0)
            def _():
                pltpu.make_async_copy(obuf.at[0], head(out, z, width), local_sem.at[5]).start()

            @pl.when(turn > 0)
            def _():
                remote(obuf.at[turn], head(out, z, width), o_sem.at[0], o_sem.at[1], {"uly": to}).start()

    for able, what in moves:
        @pl.when(able)
        def _(what=what):
            move(*what).wait_send()
    for d in range(REACH + 1):
        @pl.when(column >= d)
        def _(d=d):
            to_core(d).wait_send()
    for j in range(1, RING):
        remote(qbuf.at[j], qbuf.at[j], q_sem.at[0, j], q_sem.at[1, j], peer("uly", j)).wait_send()
    pltpu.make_async_copy(obuf.at[0], head(out, z, width), local_sem.at[5]).wait()
    got = obuf.at[pl.ds(1, RING - 1)]
    remote(got, got, o_sem.at[0], o_sem.at[1], peer("uly", 1)).wait()


def local(queries, keys, values, segments):
    rows, wide = queries.shape
    width = wide // RING
    M = GROUP * rows
    anywhere = pl.BlockSpec(memory_space=pl.ANY)
    vm = pl.BlockSpec(memory_space=pltpu.VMEM)
    out, stats = pl.pallas_call(
        ring_attend,
        out_shape=(
            jax.ShapeDtypeStruct((rows, wide), jnp.bfloat16),
            jax.ShapeDtypeStruct((8, rows), jnp.int32),
        ),
        in_specs=[vm, anywhere, anywhere, anywhere],
        out_specs=(anywhere, vm),
        scratch_shapes=[
            pltpu.VMEM((2, (REACH + 1) * COLUMN, HEAD_SIZE), jnp.bfloat16),
            pltpu.VMEM((RING, rows, width), jnp.bfloat16),
            pltpu.VMEM((RING, rows, width), jnp.bfloat16),
            pltpu.VMEM((rows, wide), jnp.bfloat16),
            pltpu.VMEM((rows, RING * HEAD_SIZE), jnp.bfloat16),
            pltpu.VMEM((RING, M, 2 * HEAD_SIZE), jnp.bfloat16),
            pltpu.VMEM((RING, HEAD_SIZE + ONES, M), jnp.float32),
            pltpu.VMEM((4, RING, 2 * NDOC, rows), jnp.float32),
            pltpu.SemaphoreType.DMA((6,)),
            pltpu.SemaphoreType.DMA((2,)),
            pltpu.SemaphoreType.DMA((2, RING)),
            pltpu.SemaphoreType.DMA((2, 4)),
            pltpu.SemaphoreType.DMA((11,)),
            pltpu.SemaphoreType.DMA((REACH + 1,)),
            pltpu.SemaphoreType.DMA((REACH + 1,)),
            pltpu.SemaphoreType.DMA((REACH + 1,)),
            pltpu.SemaphoreType.DMA((2,)),
        ],
        compiler_params=pltpu.CompilerParams(collective_id=0, has_side_effects=True, vmem_limit_bytes=56 << 20),
        name="ring_attend",
    )(segments.reshape(1, rows), queries, keys, values)
    return lax.cond(stats[0, 0] == 1, lambda *_: out, careful, queries, keys, values, segments)


def solution(mesh):
    split = Mesh(mesh.devices.reshape(4, 4, 2, mesh.shape["uly"]), AXES)
    return jax.shard_map(
        local,
        mesh=split,
        in_specs=(P(AXES, None), P(AXES, None), P(AXES, None), P(AXES)),
        out_specs=P(AXES, None),
        check_vma=False,
    )
```

```python
import functools
import jax, jax.numpy as jnp
from jax import lax
from jax.experimental import pallas as pl
from jax.experimental.pallas import tpu as pltpu
from jax.sharding import Mesh
from jax.sharding import PartitionSpec as P

HEAD_SIZE = 128
NDOC = 8
GROUP = 8
SCALE2 = 1.4426950408889634 * HEAD_SIZE ** -0.5
ONES = 16
UNIT = 512
BIG = 2048


def doc_start(info, pos):
    low = jnp.zeros_like(pos)
    for d in range(1, NDOC):
        low = jnp.where(info[d, 0] <= pos, jnp.maximum(low, info[d, 0]), low)
    return low


def contract(a, b, da, db):
    return lax.dot_general(a, b, (((da,), (db,)), ((), ())), preferred_element_type=jnp.float32)


def attend(place, info, q_ref, kv, o_ref, kbuf, vbuf, qcat, acc, top, sems):
    D = HEAD_SIZE
    piece = q_ref.shape[1]
    tiles = pieces = RING
    rows = pieces * piece
    M = GROUP * rows
    blocks = kbuf.shape[0] // tiles
    part = blocks * UNIT
    offset, stripe = place()
    shard = UNIT // pieces

    def loads(t):
        at = pl.ds(t * blocks, blocks)
        return (
            pltpu.make_async_copy(kv.at[at, pl.ds(0, UNIT)], kbuf.at[at], sems.at[0, t]),
            pltpu.make_async_copy(kv.at[at, pl.ds(UNIT, UNIT)], vbuf.at[at], sems.at[1, t]),
        )

    for t in range(tiles):
        for c in loads(t):
            c.start()

    @pl.loop(0, tiles)
    def _(t):
        base = offset + t * part
        first = base + stripe
        last = first + (pieces - 1) * shard + piece - 1
        for c in loads(t):
            c.wait()
        low = doc_start(info, first) // UNIT
        diag = base // UNIT
        lane = lax.broadcasted_iota(jnp.int32, (1, rows), 1)
        qpos = first + (lane // piece) * shard + lane % piece
        qlow = doc_start(info, qpos)

        for g in range(GROUP):
            q = q_ref[pl.ds(t * pieces, pieces), :, g * D:(g + 1) * D].reshape(rows, D).astype(jnp.float32) * SCALE2
            high = q.astype(jnp.bfloat16)
            at = slice(g * rows, (g + 1) * rows)
            qcat[at, :D] = high
            qcat[at, D:] = (q - high.astype(jnp.float32)).astype(jnp.bfloat16)
        acc[...] = jnp.zeros_like(acc)

        def allowed(at, size):
            kpos = at + lax.broadcasted_iota(jnp.int32, (size, rows), 0)
            return (kpos <= qpos) & (kpos >= qlow)

        def masked(p, m):
            return jnp.concatenate(
                [jnp.where(m, p[:, g * rows:(g + 1) * rows], 0.0) for g in range(p.shape[1] // rows)], axis=1)

        def step(at, size):
            k = kbuf[pl.ds(at, size // UNIT)].reshape(size, D)
            v = vbuf[pl.ds(at, size // UNIT)].reshape(size, D)
            kk = jnp.concatenate([k, k], axis=1)
            vv = jnp.concatenate([v, jnp.ones((size, ONES), v.dtype)], axis=1)
            p = masked(jnp.exp2(contract(kk, qcat[...], 1, 1)), allowed(at * UNIT, size))
            acc[...] += contract(vv, p.astype(jnp.bfloat16), 0, 0)

        units = diag + 1 - low
        per = BIG // UNIT
        big = units // per

        @pl.loop(0, big)
        def _(n):
            step(low + n * per, BIG)

        size = BIG // 2
        done = low + big * per
        while size >= UNIT:
            some = (units // (size // UNIT)) % 2

            @pl.when(some == 1)
            def _(done=done, size=size):
                step(done, size)

            done = done + some * (size // UNIT)
            size //= 2

        total = acc[D:D + 8, :]
        good = jnp.min(jnp.where((total > 2.0 ** -60) & (total < 2.0 ** 118), 1.0, 0.0))

        @pl.when(good < 0.5)
        def _():
            top[...] = jnp.full_like(top, -1e30)
            acc[...] = jnp.zeros_like(acc)

            def scores(n, g):
                q = q_ref[pl.ds(t * pieces, pieces), :, pl.ds(pl.multiple_of(g * D, D), D)].reshape(rows, D)
                m = allowed(n * UNIT, UNIT)
                return jnp.where(m, contract(kbuf[n], q, 1, 1) * SCALE2, -1e30), m

            @pl.loop(low, diag + 1)
            def _(n):
                @pl.loop(0, GROUP)
                def _(g):
                    at = pl.ds(pl.multiple_of(g * rows, rows), rows)
                    s, _ = scores(n, g)
                    top[:, at] = jnp.maximum(top[:, at], jnp.max(s, axis=0, keepdims=True))

            @pl.loop(low, diag + 1)
            def _(n):
                v = vbuf[n]
                vv = jnp.concatenate([v, jnp.ones((UNIT, ONES), v.dtype)], axis=1)

                @pl.loop(0, GROUP)
                def _(g):
                    at = pl.ds(pl.multiple_of(g * rows, rows), rows)
                    s, m = scores(n, g)
                    p = jnp.where(m, jnp.exp2(s - top[:1, at]), 0.0)
                    acc[:, at] += contract(vv, p.astype(jnp.bfloat16), 0, 0)

        for g in range(GROUP):
            at = slice(g * rows, (g + 1) * rows)
            out = acc[:D, at] / acc[D:D + 1, at]
            o_ref[pl.ds(t * pieces, pieces), :, g * D:(g + 1) * D] = out.T.astype(jnp.bfloat16).reshape(pieces, piece, D)


def place():
    return (
        lax.axis_index(("blk_1", "blk_2")) * UNIT,
        lax.axis_index("blk_0") * (UNIT // RING // RING),
    )


def attention(starts, q, kv, place=place):
    M = GROUP * RING * q.shape[1]
    vm = pl.BlockSpec(memory_space=pltpu.VMEM)
    half = (kv.shape[0], UNIT, HEAD_SIZE)
    return pl.pallas_call(
        functools.partial(attend, place),
        out_shape=jax.ShapeDtypeStruct(q.shape, jnp.bfloat16),
        in_specs=[pl.BlockSpec(memory_space=pltpu.SMEM), vm, pl.BlockSpec(memory_space=pl.ANY)],
        out_specs=vm,
        scratch_shapes=[
            pltpu.VMEM(half, jnp.bfloat16),
            pltpu.VMEM(half, jnp.bfloat16),
            pltpu.VMEM((M, 2 * HEAD_SIZE), jnp.bfloat16),
            pltpu.VMEM((HEAD_SIZE + ONES, M), jnp.float32),
            pltpu.VMEM((8, M), jnp.float32),
            pltpu.SemaphoreType.DMA((2, RING)),
        ],
        compiler_params=pltpu.CompilerParams(vmem_limit_bytes=56 << 20),
        name="attend",
    )(starts, q, kv)


AXES = ("blk_0", "blk_1", "blk_2", "uly")
RING = 4
K_ROWS = UNIT
FIRST_ROWS = 768


def coordinates():
    return {axis: lax.axis_index(axis) for axis in AXES}


def shifted(at, axis, by):
    size = 2 if axis == "blk_2" else RING
    return lax.rem(at[axis] + (by + size), size)


def greet(peers):
    barrier = pltpu.get_barrier_semaphore()
    for peer in peers:
        pl.semaphore_signal(barrier, inc=1, device_id=peer, device_id_type=pl.DeviceIdType.MESH)
    pl.semaphore_wait(barrier, len(peers))


def remote(src, dst, send, recv, peer):
    return pltpu.make_async_remote_copy(
        src_ref=src, dst_ref=dst, send_sem=send, recv_sem=recv, device_id=peer,
        device_id_type=pl.DeviceIdType.MESH)


def square_peers(at):
    return [
        {"blk_0": shifted(at, "blk_0", i), "uly": shifted(at, "uly", j)}
        for i in range(RING) for j in range(RING) if i or j
    ]


def exchange(seg, q_in, k_in, v_in, q_out, kv, count_out, counts, own_sem, q_sem, z_sem, c_sem, stream_send, stream_recv, core_sem):
    D = HEAD_SIZE
    at = coordinates()
    x, y, c, z = (at[a] for a in AXES)
    rows = q_in.shape[0]
    piece = rows // RING
    width = q_in.shape[1] // RING
    greet(square_peers(at) + [{"blk_1": shifted(at, "blk_1", j)} for j in range(1, RING)] + [{"blk_2": 1 - c}])

    def block(i, j):
        return (shifted(at, "blk_0", i) * RING + shifted(at, "blk_1", j)) * 2 + c

    me = block(0, 0)
    mine = pl.ds(pl.multiple_of(z * rows, rows), rows)
    low = pl.ds(pl.multiple_of(UNIT + z * rows, rows), rows)

    def head(ref, h):
        return ref.at[:, pl.ds(pl.multiple_of(h * D, D), D)]

    own = [
        pltpu.make_async_copy(head(k_in, z), kv.at[me, mine], own_sem.at[0]),
        pltpu.make_async_copy(head(v_in, z), kv.at[me, low], own_sem.at[1]),
    ]
    for copy in own:
        copy.start()
    for j in range(1, RING):
        to = shifted(at, "uly", j)
        remote(head(k_in, to), kv.at[me, mine], z_sem.at[0], z_sem.at[1], {"uly": to}).start()
        remote(head(v_in, to), kv.at[me, low], z_sem.at[0], z_sem.at[1], {"uly": to}).start()

    def q_part(i, j):
        return q_in.at[pl.ds(pl.multiple_of(i * piece, piece), piece), pl.ds(pl.multiple_of(j * width, width), width)]

    q_own = pltpu.make_async_copy(q_part(x, z), q_out.at[x * RING + z], own_sem.at[2])
    q_own.start()

    def send_counts(phase, axis, value):
        size = 2 if axis == "blk_2" else RING
        counts[phase, 0] = value
        for j in range(1, size):
            remote(counts.at[phase, 0], counts.at[phase, size - j], c_sem.at[0, phase], c_sem.at[1, phase],
                   {axis: shifted(at, axis, j)}).start()

    def sum_counts(phase, axis):
        size = 2 if axis == "blk_2" else RING
        got = counts.at[phase, pl.ds(1, size - 1)]
        remote(got, got, c_sem.at[0, phase], c_sem.at[1, phase], {axis: shifted(at, axis, 1)}).wait()
        total = counts[phase, 0]
        for j in range(1, size):
            total = total + counts[phase, j]
        return total

    docs = lax.broadcasted_iota(jnp.int32, (NDOC, seg.shape[1]), 0)
    send_counts(0, "uly", jnp.where(seg[...] < docs, 1, 0))

    for peer in square_peers(at):
        i, j = (peer["blk_0"], peer["uly"])
        remote(q_part(i, j), q_out.at[x * RING + z], q_sem.at[0], q_sem.at[1], peer).start()

    for copy in own:
        copy.wait()
    got = kv.at[0, pl.ds(0, 2 * (RING - 1) * rows)]
    remote(got, got, z_sem.at[0], z_sem.at[1], {"uly": shifted(at, "uly", 1)}).wait()

    streams = (
        (0, 0, FIRST_ROWS, "blk_0", "blk_1"),
        (1, FIRST_ROWS, 2 * UNIT - FIRST_ROWS, "blk_1", "blk_0"),
    )
    order = (0, -1, 1, 2)

    def region(stream, i, j, half=None):
        _, start, size, first, _ = stream
        if half is not None:
            size //= 2
            start += half * size
        return kv.at[block(i, j) if first == "blk_0" else block(j, i), pl.ds(start, size)]

    def ring_copy(stream, what, axis, by, slot):
        return remote(what, what, stream_send.at[stream[0]], stream_recv.at[stream[0], slot], {axis: shifted(at, axis, by)})

    def to_core(what):
        remote(what, what, core_sem.at[0], core_sem.at[1], {"blk_2": 1 - c}).start()

    def spread(stream, axis, slot, pick):
        ring_copy(stream, pick(0), axis, 1, slot).start()
        ring_copy(stream, pick(0), axis, -1, slot + 1).start()

    def relay(stream, axis, slot, pick):
        ring_copy(stream, pick(-1), axis, 1, slot).wait_recv()
        ring_copy(stream, pick(-1, 0), axis, 1, slot + 2).start()
        ring_copy(stream, pick(1), axis, -1, slot + 1).wait_recv()
        ring_copy(stream, pick(1, 1), axis, -1, slot + 3).start()

    def settle(stream, axis, slot, pick):
        ring_copy(stream, pick(2, 0), axis, 1, slot + 2).wait_recv()
        ring_copy(stream, pick(2, 1), axis, -1, slot + 3).wait_recv()

    def along_first(stream):
        return lambda i, half=None: region(stream, i, 0, half)

    def along_second(stream, i):
        return lambda j, half=None: region(stream, i, j, half)

    for s in streams:
        spread(s, s[3], 0, along_first(s))
    for s in streams:
        spread(s, s[4], 4, along_second(s, 0))
    to_core(kv.at[me])
    send_counts(1, "blk_0", sum_counts(0, "uly"))
    for s in streams:
        relay(s, s[3], 0, along_first(s))
        for n in (1, 2):
            spread(s, s[4], 4 + 4 * n, along_second(s, order[n]))
            to_core(region(s, order[n], 0))
    send_counts(2, "blk_1", sum_counts(1, "blk_0"))
    for s in streams:
        relay(s, s[4], 4, along_second(s, 0))
        to_core(region(s, 0, -1))
        to_core(region(s, 0, 1))
    for s in streams:
        settle(s, s[3], 0, along_first(s))
        spread(s, s[4], 16, along_second(s, 2))
        to_core(region(s, 2, 0))
    send_counts(3, "blk_2", sum_counts(2, "blk_1"))
    for n in (1, 2, 3):
        for s in streams:
            settle(s, s[4], 4 * n, along_second(s, order[n - 1]))
            to_core(region(s, order[n - 1], 2))
            relay(s, s[4], 4 + 4 * n, along_second(s, order[n]))
            to_core(region(s, order[n], -1))
            to_core(region(s, order[n], 1))
    count_out[...] = jnp.broadcast_to(jnp.sum(sum_counts(3, "blk_2"), axis=1, keepdims=True), count_out.shape)
    for s in streams:
        settle(s, s[4], 16, along_second(s, 2))
        to_core(region(s, 2, 2))
    for s in streams:
        sent = kv.at[pl.ds(0, 15), pl.ds(s[1], s[2])]
        ring_copy(s, sent, s[3], 1, 0).wait_send()
    half = kv.at[pl.ds(0, 16)]
    remote(half, half, core_sem.at[0], core_sem.at[1], {"blk_2": 1 - c}).wait()
    q_own.wait()
    most = q_out.at[pl.ds(0, RING * RING - 1)]
    remote(most, most, q_sem.at[0], q_sem.at[1], {"uly": shifted(at, "uly", 1)}).wait()


def give_back(o_in, out, own_sem, sem):
    at = coordinates()
    x, z = at["blk_0"], at["uly"]
    piece, width = o_in.shape[1:]
    peers = square_peers(at)
    greet(peers)
    here = out.at[pl.ds(pl.multiple_of(x * piece, piece), piece), pl.ds(pl.multiple_of(z * width, width), width)]
    own = pltpu.make_async_copy(o_in.at[x * RING + z], here, own_sem)
    for peer in peers:
        remote(o_in.at[peer["blk_0"] * RING + peer["uly"]], here, sem.at[0], sem.at[1], peer).start()
    own.start()
    own.wait()
    most = o_in.at[pl.ds(0, RING * RING - 1)]
    remote(most, most, sem.at[0], sem.at[1], peers[0]).wait()


def careful(queries, keys, values, segments):
    rows, wide = queries.shape
    piece, width = rows // RING, wide // RING
    anywhere = pl.BlockSpec(memory_space=pl.ANY)
    vm = pl.BlockSpec(memory_space=pltpu.VMEM)
    q, kv, starts = pl.pallas_call(
        exchange,
        out_shape=(
            jax.ShapeDtypeStruct((RING * RING, piece, width), jnp.bfloat16),
            jax.ShapeDtypeStruct((2 * RING * RING, 2 * UNIT, HEAD_SIZE), jnp.bfloat16),
            jax.ShapeDtypeStruct((NDOC, 128), jnp.int32),
        ),
        in_specs=[vm, anywhere, anywhere, anywhere],
        out_specs=(anywhere, anywhere, vm),
        scratch_shapes=[
            pltpu.VMEM((4, RING, NDOC, rows), jnp.int32),
            pltpu.SemaphoreType.DMA((3,)),
            pltpu.SemaphoreType.DMA((2,)),
            pltpu.SemaphoreType.DMA((2,)),
            pltpu.SemaphoreType.DMA((2, 4)),
            pltpu.SemaphoreType.DMA((2,)),
            pltpu.SemaphoreType.DMA((2, 20)),
            pltpu.SemaphoreType.DMA((2,)),
        ],
        compiler_params=pltpu.CompilerParams(collective_id=1, has_side_effects=True),
        name="exchange",
    )(segments.reshape(1, rows), queries, keys, values)
    out = attention(starts, q, kv)
    return pl.pallas_call(
        give_back,
        out_shape=jax.ShapeDtypeStruct((rows, wide), jnp.bfloat16),
        in_specs=[anywhere],
        out_specs=anywhere,
        scratch_shapes=[pltpu.SemaphoreType.DMA, pltpu.SemaphoreType.DMA((2,))],
        compiler_params=pltpu.CompilerParams(collective_id=2, has_side_effects=True),
        name="give_back",
    )(out)


COLUMN = 2 * UNIT
REACH = 8
CHUNK = 2080
CHUNKS = 4
WAITS = (
    (0, (1, 2), (0, 1, 2), 3),
    (2, (3,), (), 0),
    (3, (8,), (), 3),
    (4, (), (3, 4), 0),
    (6, (5, 6), (), 0),
    (7, (7,), (), 0),
    (8, (), (5, 6), 0),
    (9, (), (7, 8), 0),
)
LIMIT = 100.0


def ring_attend(seg, q_in, k_in, v_in, out, stats_out, kv, qbuf, obuf, qv, kv_own, qcat, acc, stats,
                local_sem, bar_z, q_sem, s_sem, send_sem, recv_sem, core_send, core_recv, o_sem):
    D = HEAD_SIZE
    x, y, c, z = (lax.axis_index(a) for a in AXES)
    column = x * RING + y
    rows = q_in.shape[0]
    width = q_in.shape[1] // RING

    def peer(axis, by):
        size = 2 if axis == "blk_2" else RING
        return {axis: lax.rem(lax.axis_index(axis) + by, size)}

    def group(phase):
        if phase == 0:
            return [peer("uly", j) for j in range(1, RING)]
        if phase == 2:
            return [peer("blk_0", j) for j in range(1, RING)]
        return [{**peer("blk_1", j % RING), **peer("blk_2", j // RING)} for j in range(1, 2 * RING)]

    greet(group(0) + group(1) + group(2))

    def place(d, core):
        return pl.ds(pl.multiple_of((REACH - d) * COLUMN + core * UNIT, UNIT), UNIT)

    mine = pl.ds(pl.multiple_of(REACH * COLUMN + c * UNIT + z * rows, rows), rows)

    def head(ref, h, size):
        return ref.at[:, pl.ds(pl.multiple_of(h * size, size), size)]

    for j in (1, 3, 2):
        to = peer("uly", j)
        remote(head(k_in, to["uly"], D), kv.at[0, mine], bar_z.at[0], bar_z.at[1], to).start()
        remote(head(v_in, to["uly"], D), kv.at[1, mine], bar_z.at[0], bar_z.at[1], to).start()
    own = [
        pltpu.make_async_copy(head(k_in, z, D), kv.at[0, mine], local_sem.at[0]),
        pltpu.make_async_copy(head(v_in, z, D), kv.at[1, mine], local_sem.at[1]),
        pltpu.make_async_copy(head(q_in, z, width), qbuf.at[0], local_sem.at[2]),
        pltpu.make_async_copy(q_in, qv, local_sem.at[3]),
        pltpu.make_async_copy(k_in, kv_own, local_sem.at[4]),
    ]
    for copy in own:
        copy.start()
    @pl.loop(1, REACH + 1)
    def _(d):
        @pl.when(column < d)
        def _():
            at = pl.ds(pl.multiple_of((REACH - d) * COLUMN, COLUMN), COLUMN)
            kv[0, at] = jnp.zeros((COLUMN, D), kv.dtype)
            kv[1, at] = jnp.zeros((COLUMN, D), kv.dtype)

    own[3].wait()
    own[4].wait()

    def longest(ref):
        most = jnp.zeros((rows, 1), jnp.float32)
        for h in range(ref.shape[1] // D):
            a = ref[:, h * D:(h + 1) * D].astype(jnp.float32)
            most = jnp.maximum(most, jnp.sum(a * a, axis=1, keepdims=True))
        return jnp.broadcast_to(jnp.max(most, axis=0, keepdims=True), (1, rows))

    kind = lax.broadcasted_iota(jnp.int32, (2 * NDOC, rows), 0)
    before = jnp.where(seg[...] < kind, 1.0, 0.0)
    before = jnp.where(kind == NDOC, longest(qv), jnp.where(kind > NDOC, longest(kv_own), before))

    def send_stats(phase, value):
        stats[phase, 0] = value
        to = group(phase)
        for n, target in enumerate(to):
            slot = (n + 1) % RING + (n + 1) // RING * RING
            slot = (RING - slot % RING) % RING + slot // RING * RING
            remote(stats.at[phase, 0], stats.at[phase, slot], s_sem.at[0, phase], s_sem.at[1, phase], target).start()

    def sum_stats(phase):
        size = len(group(phase)) + 1
        got = stats.at[phase, pl.ds(1, size - 1)]
        remote(got, got, s_sem.at[0, phase], s_sem.at[1, phase], group(phase)[0]).wait()
        total = stats[phase, 0]
        for j in range(1, size):
            other = stats[phase, j]
            total = jnp.where(kind < NDOC, total + other, jnp.maximum(total, other))
        return total

    send_stats(0, before)
    own[0].wait()
    own[1].wait()
    got = kv.at[0, pl.ds(0, 2 * (RING - 1) * rows)]
    remote(got, got, bar_z.at[0], bar_z.at[1], peer("uly", 1)).wait()
    for j in (1, 3, 2):
        to = peer("uly", j)
        remote(head(q_in, to["uly"], width), qbuf.at[RING - j], q_sem.at[0, j], q_sem.at[1, RING - j], to).start()


    def move(n, from_d, to_d, to):
        return remote(kv.at[:, place(from_d, c)], kv.at[:, place(to_d, c)], send_sem.at[n], recv_sem.at[to_d], to)

    moves = []

    def start_if(able, *what):
        moves.append((able, what))

        @pl.when(able)
        def _():
            move(*what).start()

    def received(d):
        @pl.when(column >= d)
        def _():
            move(0, d, d, {"blk_1": y}).wait_recv()
            to_core(d).start()

    def to_core(d):
        what = kv.at[:, place(d, c)]
        return remote(what, what, core_send.at[d], core_recv.at[d], {"blk_2": 1 - c})

    def from_core(d):
        @pl.when(column >= d)
        def _():
            to_core(d).wait_recv()

    later = []

    def start_later(able, *what):
        moves.append((able, what))
        later.append((able, what))

    def flush(count):
        for _ in range(count):
            able, what = later.pop(0)

            @pl.when(able)
            def _(what=what):
                move(*what).start()

    send_stats(1, sum_stats(0))
    for j in (1, 2, 3):
        start_if(y + j < RING, 1 + j, 0, j, peer("blk_1", j))
    start_if(x < 3, 0, 0, 4, peer("blk_0", 1))
    to_core(0).start()
    send_stats(2, sum_stats(1))
    received(4)
    start_if((x >= 1) & (x < 3), 1, 4, 8, peer("blk_0", 1))
    for j in (1, 2, 3):
        start_if((x >= 1) & (y >= j), 4 + j, 4, 4 - j, peer("blk_1", RING - j))
    for j in (1, 2, 3):
        start_later((x >= 1) & (y + j < RING), 10 + j, 4, 4 + j, peer("blk_1", j))
    for j in (1, 2, 3):
        start_later((x >= 2) & (y >= j), 7 + j, 8, 8 - j, peer("blk_1", RING - j))
    final = sum_stats(2)
    reach = final[NDOC:NDOC + 1] * final[NDOC + 1:NDOC + 2] * SCALE2 ** 2
    stats_out[...] = jnp.broadcast_to(jnp.where(reach < LIMIT ** 2, 1, 0), stats_out.shape)
    starts = jnp.sum(final[:NDOC], axis=1, keepdims=True).astype(jnp.int32)
    starts = jnp.broadcast_to(starts, (NDOC, rows))
    own[2].wait()

    @pl.loop(0, RING * CHUNKS)
    def _(n):
        early = n < 2 * RING
        last = (n - 2 * RING) // 2
        turn = jnp.where(early, n % RING, jnp.where(last == 0, 2, jnp.where(last == RING - 1, 0, 2 * last - 1)))
        chunk = jnp.where(early, n // RING, 2 + n % 2)
        to = lax.rem(z + turn, RING)

        for at_step, arrivals, crossed, count in WAITS:
            @pl.when(n == at_step)
            def _(arrivals=arrivals, crossed=crossed, count=count):
                for d in arrivals:
                    received(d)
                for d in crossed:
                    from_core(d)
                flush(count)

        @pl.when(chunk == 0)
        def _():
            @pl.when(turn > 0)
            def _():
                remote(qbuf.at[turn], qbuf.at[turn], q_sem.at[0, turn], q_sem.at[1, turn], {"uly": to}).wait_recv()

            for g in range(GROUP):
                q = qbuf[turn, :, g * D:(g + 1) * D].astype(jnp.float32) * SCALE2
                high = q.astype(jnp.bfloat16)
                at = slice(g * rows, (g + 1) * rows)
                qcat[turn, at, :D] = high
                qcat[turn, at, D:] = (q - high.astype(jnp.float32)).astype(jnp.bfloat16)
            acc[turn] = jnp.zeros(acc.shape[1:], acc.dtype)

        qpos = column * COLUMN + c * UNIT + to * rows + lax.broadcasted_iota(jnp.int32, (1, rows), 1)
        qlow = jnp.zeros_like(qpos)
        for d in range(1, NDOC):
            qlow = jnp.where(starts[d:d + 1] <= qpos, jnp.maximum(qlow, starts[d:d + 1]), qlow)
        first = c * UNIT + to * rows + (CHUNKS - 1 - chunk) * CHUNK
        at = pl.ds(pl.multiple_of(first, 32), CHUNK)
        kpos = (column - REACH) * COLUMN + first + lax.broadcasted_iota(jnp.int32, (CHUNK, rows), 0)
        allowed = (kpos <= qpos) & (kpos >= qlow)
        k = kv[0, at]
        v = kv[1, at]
        kk = jnp.concatenate([k, k], axis=1)
        vv = jnp.concatenate([v, jnp.ones((CHUNK, ONES), v.dtype)], axis=1)
        p = jnp.exp2(contract(kk, qcat[turn], 1, 1))
        p = jnp.concatenate([jnp.where(allowed, p[:, g * rows:(g + 1) * rows], 0.0) for g in range(GROUP)], axis=1)
        acc[turn] += contract(vv, p.astype(jnp.bfloat16), 0, 0)

        @pl.when(chunk == CHUNKS - 1)
        def _():
            for g in range(GROUP):
                a = slice(g * rows, (g + 1) * rows)
                o = acc[turn, :D, a] / acc[turn, D:D + 1, a]
                obuf[turn, :, g * D:(g + 1) * D] = o.T.astype(jnp.bfloat16)

            @pl.when(turn == 0)
            def _():
                pltpu.make_async_copy(obuf.at[0], head(out, z, width), local_sem.at[5]).start()

            @pl.when(turn > 0)
            def _():
                remote(obuf.at[turn], head(out, z, width), o_sem.at[0], o_sem.at[1], {"uly": to}).start()

    for able, what in moves:
        @pl.when(able)
        def _(what=what):
            move(*what).wait_send()
    for d in range(REACH + 1):
        @pl.when(column >= d)
        def _(d=d):
            to_core(d).wait_send()
    for j in range(1, RING):
        remote(qbuf.at[j], qbuf.at[j], q_sem.at[0, j], q_sem.at[1, j], peer("uly", j)).wait_send()
    pltpu.make_async_copy(obuf.at[0], head(out, z, width), local_sem.at[5]).wait()
    got = obuf.at[pl.ds(1, RING - 1)]
    remote(got, got, o_sem.at[0], o_sem.at[1], peer("uly", 1)).wait()


def local(queries, keys, values, segments):
    rows, wide = queries.shape
    width = wide // RING
    M = GROUP * rows
    anywhere = pl.BlockSpec(memory_space=pl.ANY)
    vm = pl.BlockSpec(memory_space=pltpu.VMEM)
    out, stats = pl.pallas_call(
        ring_attend,
        out_shape=(
            jax.ShapeDtypeStruct((rows, wide), jnp.bfloat16),
            jax.ShapeDtypeStruct((8, rows), jnp.int32),
        ),
        in_specs=[vm, anywhere, anywhere, anywhere],
        out_specs=(anywhere, vm),
        scratch_shapes=[
            pltpu.VMEM((2, (REACH + 1) * COLUMN, HEAD_SIZE), jnp.bfloat16),
            pltpu.VMEM((RING, rows, width), jnp.bfloat16),
            pltpu.VMEM((RING, rows, width), jnp.bfloat16),
            pltpu.VMEM((rows, wide), jnp.bfloat16),
            pltpu.VMEM((rows, RING * HEAD_SIZE), jnp.bfloat16),
            pltpu.VMEM((RING, M, 2 * HEAD_SIZE), jnp.bfloat16),
            pltpu.VMEM((RING, HEAD_SIZE + ONES, M), jnp.float32),
            pltpu.VMEM((3, 2 * RING, 2 * NDOC, rows), jnp.float32),
            pltpu.SemaphoreType.DMA((6,)),
            pltpu.SemaphoreType.DMA((2,)),
            pltpu.SemaphoreType.DMA((2, RING)),
            pltpu.SemaphoreType.DMA((2, 4)),
            pltpu.SemaphoreType.DMA((14,)),
            pltpu.SemaphoreType.DMA((REACH + 1,)),
            pltpu.SemaphoreType.DMA((REACH + 1,)),
            pltpu.SemaphoreType.DMA((REACH + 1,)),
            pltpu.SemaphoreType.DMA((2,)),
        ],
        compiler_params=pltpu.CompilerParams(collective_id=0, has_side_effects=True, vmem_limit_bytes=56 << 20),
        name="ring_attend",
    )(segments.reshape(1, rows), queries, keys, values)
    return lax.cond(stats[0, 0] == 1, lambda *_: out, careful, queries, keys, values, segments)


def solution(mesh):
    split = Mesh(mesh.devices.reshape(4, 4, 2, mesh.shape["uly"]), AXES)
    return jax.shard_map(
        local,
        mesh=split,
        in_specs=(P(AXES, None), P(AXES, None), P(AXES, None), P(AXES)),
        out_specs=P(AXES, None),
        check_vma=False,
    )
```

```python
import functools
import jax, jax.numpy as jnp
from jax import lax
from jax.experimental import pallas as pl
from jax.experimental.pallas import tpu as pltpu
from jax.sharding import Mesh
from jax.sharding import PartitionSpec as P

HEAD_SIZE = 128
NDOC = 8
GROUP = 8
SCALE2 = 1.4426950408889634 * HEAD_SIZE ** -0.5
ONES = 16
UNIT = 512
BIG = 2048


def doc_start(info, pos):
    low = jnp.zeros_like(pos)
    for d in range(1, NDOC):
        low = jnp.where(info[d, 0] <= pos, jnp.maximum(low, info[d, 0]), low)
    return low


def contract(a, b, da, db):
    return lax.dot_general(a, b, (((da,), (db,)), ((), ())), preferred_element_type=jnp.float32)


def attend(place, info, q_ref, kv, o_ref, kbuf, vbuf, qcat, acc, top, sems):
    D = HEAD_SIZE
    piece = q_ref.shape[1]
    tiles = pieces = RING
    rows = pieces * piece
    M = GROUP * rows
    blocks = kbuf.shape[0] // tiles
    part = blocks * UNIT
    offset, stripe = place()
    shard = UNIT // pieces

    def loads(t):
        at = pl.ds(t * blocks, blocks)
        return (
            pltpu.make_async_copy(kv.at[at, pl.ds(0, UNIT)], kbuf.at[at], sems.at[0, t]),
            pltpu.make_async_copy(kv.at[at, pl.ds(UNIT, UNIT)], vbuf.at[at], sems.at[1, t]),
        )

    for t in range(tiles):
        for c in loads(t):
            c.start()

    @pl.loop(0, tiles)
    def _(t):
        base = offset + t * part
        first = base + stripe
        last = first + (pieces - 1) * shard + piece - 1
        for c in loads(t):
            c.wait()
        low = doc_start(info, first) // UNIT
        diag = base // UNIT
        lane = lax.broadcasted_iota(jnp.int32, (1, rows), 1)
        qpos = first + (lane // piece) * shard + lane % piece
        qlow = doc_start(info, qpos)

        for g in range(GROUP):
            q = q_ref[pl.ds(t * pieces, pieces), :, g * D:(g + 1) * D].reshape(rows, D).astype(jnp.float32) * SCALE2
            high = q.astype(jnp.bfloat16)
            at = slice(g * rows, (g + 1) * rows)
            qcat[at, :D] = high
            qcat[at, D:] = (q - high.astype(jnp.float32)).astype(jnp.bfloat16)
        acc[...] = jnp.zeros_like(acc)

        def allowed(at, size):
            kpos = at + lax.broadcasted_iota(jnp.int32, (size, rows), 0)
            return (kpos <= qpos) & (kpos >= qlow)

        def masked(p, m):
            return jnp.concatenate(
                [jnp.where(m, p[:, g * rows:(g + 1) * rows], 0.0) for g in range(p.shape[1] // rows)], axis=1)

        def step(at, size):
            k = kbuf[pl.ds(at, size // UNIT)].reshape(size, D)
            v = vbuf[pl.ds(at, size // UNIT)].reshape(size, D)
            kk = jnp.concatenate([k, k], axis=1)
            vv = jnp.concatenate([v, jnp.ones((size, ONES), v.dtype)], axis=1)
            p = masked(jnp.exp2(contract(kk, qcat[...], 1, 1)), allowed(at * UNIT, size))
            acc[...] += contract(vv, p.astype(jnp.bfloat16), 0, 0)

        units = diag + 1 - low
        per = BIG // UNIT
        big = units // per

        @pl.loop(0, big)
        def _(n):
            step(low + n * per, BIG)

        size = BIG // 2
        done = low + big * per
        while size >= UNIT:
            some = (units // (size // UNIT)) % 2

            @pl.when(some == 1)
            def _(done=done, size=size):
                step(done, size)

            done = done + some * (size // UNIT)
            size //= 2

        total = acc[D:D + 8, :]
        good = jnp.min(jnp.where((total > 2.0 ** -60) & (total < 2.0 ** 118), 1.0, 0.0))

        @pl.when(good < 0.5)
        def _():
            top[...] = jnp.full_like(top, -1e30)
            acc[...] = jnp.zeros_like(acc)

            def scores(n, g):
                q = q_ref[pl.ds(t * pieces, pieces), :, pl.ds(pl.multiple_of(g * D, D), D)].reshape(rows, D)
                m = allowed(n * UNIT, UNIT)
                return jnp.where(m, contract(kbuf[n], q, 1, 1) * SCALE2, -1e30), m

            @pl.loop(low, diag + 1)
            def _(n):
                @pl.loop(0, GROUP)
                def _(g):
                    at = pl.ds(pl.multiple_of(g * rows, rows), rows)
                    s, _ = scores(n, g)
                    top[:, at] = jnp.maximum(top[:, at], jnp.max(s, axis=0, keepdims=True))

            @pl.loop(low, diag + 1)
            def _(n):
                v = vbuf[n]
                vv = jnp.concatenate([v, jnp.ones((UNIT, ONES), v.dtype)], axis=1)

                @pl.loop(0, GROUP)
                def _(g):
                    at = pl.ds(pl.multiple_of(g * rows, rows), rows)
                    s, m = scores(n, g)
                    p = jnp.where(m, jnp.exp2(s - top[:1, at]), 0.0)
                    acc[:, at] += contract(vv, p.astype(jnp.bfloat16), 0, 0)

        for g in range(GROUP):
            at = slice(g * rows, (g + 1) * rows)
            out = acc[:D, at] / acc[D:D + 1, at]
            o_ref[pl.ds(t * pieces, pieces), :, g * D:(g + 1) * D] = out.T.astype(jnp.bfloat16).reshape(pieces, piece, D)


def place():
    return (
        lax.axis_index(("blk_1", "blk_2")) * UNIT,
        lax.axis_index("blk_0") * (UNIT // RING // RING),
    )


def attention(starts, q, kv, place=place):
    M = GROUP * RING * q.shape[1]
    vm = pl.BlockSpec(memory_space=pltpu.VMEM)
    half = (kv.shape[0], UNIT, HEAD_SIZE)
    return pl.pallas_call(
        functools.partial(attend, place),
        out_shape=jax.ShapeDtypeStruct(q.shape, jnp.bfloat16),
        in_specs=[pl.BlockSpec(memory_space=pltpu.SMEM), vm, pl.BlockSpec(memory_space=pl.ANY)],
        out_specs=vm,
        scratch_shapes=[
            pltpu.VMEM(half, jnp.bfloat16),
            pltpu.VMEM(half, jnp.bfloat16),
            pltpu.VMEM((M, 2 * HEAD_SIZE), jnp.bfloat16),
            pltpu.VMEM((HEAD_SIZE + ONES, M), jnp.float32),
            pltpu.VMEM((8, M), jnp.float32),
            pltpu.SemaphoreType.DMA((2, RING)),
        ],
        compiler_params=pltpu.CompilerParams(vmem_limit_bytes=56 << 20),
        name="attend",
    )(starts, q, kv)


AXES = ("blk_0", "blk_1", "blk_2", "uly")
RING = 4
K_ROWS = UNIT
FIRST_ROWS = 768


def coordinates():
    return {axis: lax.axis_index(axis) for axis in AXES}


def shifted(at, axis, by):
    size = 2 if axis == "blk_2" else RING
    return lax.rem(at[axis] + (by + size), size)


def greet(peers):
    barrier = pltpu.get_barrier_semaphore()
    for peer in peers:
        pl.semaphore_signal(barrier, inc=1, device_id=peer, device_id_type=pl.DeviceIdType.MESH)
    pl.semaphore_wait(barrier, len(peers))


def remote(src, dst, send, recv, peer):
    return pltpu.make_async_remote_copy(
        src_ref=src, dst_ref=dst, send_sem=send, recv_sem=recv, device_id=peer,
        device_id_type=pl.DeviceIdType.MESH)


def square_peers(at):
    return [
        {"blk_0": shifted(at, "blk_0", i), "uly": shifted(at, "uly", j)}
        for i in range(RING) for j in range(RING) if i or j
    ]


def exchange(seg, q_in, k_in, v_in, q_out, kv, count_out, counts, own_sem, q_sem, z_sem, c_sem, stream_send, stream_recv, core_sem):
    D = HEAD_SIZE
    at = coordinates()
    x, y, c, z = (at[a] for a in AXES)
    rows = q_in.shape[0]
    piece = rows // RING
    width = q_in.shape[1] // RING
    greet(square_peers(at) + [{"blk_1": shifted(at, "blk_1", j)} for j in range(1, RING)] + [{"blk_2": 1 - c}])

    def block(i, j):
        return (shifted(at, "blk_0", i) * RING + shifted(at, "blk_1", j)) * 2 + c

    me = block(0, 0)
    mine = pl.ds(pl.multiple_of(z * rows, rows), rows)
    low = pl.ds(pl.multiple_of(UNIT + z * rows, rows), rows)

    def head(ref, h):
        return ref.at[:, pl.ds(pl.multiple_of(h * D, D), D)]

    own = [
        pltpu.make_async_copy(head(k_in, z), kv.at[me, mine], own_sem.at[0]),
        pltpu.make_async_copy(head(v_in, z), kv.at[me, low], own_sem.at[1]),
    ]
    for copy in own:
        copy.start()
    for j in range(1, RING):
        to = shifted(at, "uly", j)
        remote(head(k_in, to), kv.at[me, mine], z_sem.at[0], z_sem.at[1], {"uly": to}).start()
        remote(head(v_in, to), kv.at[me, low], z_sem.at[0], z_sem.at[1], {"uly": to}).start()

    def q_part(i, j):
        return q_in.at[pl.ds(pl.multiple_of(i * piece, piece), piece), pl.ds(pl.multiple_of(j * width, width), width)]

    q_own = pltpu.make_async_copy(q_part(x, z), q_out.at[x * RING + z], own_sem.at[2])
    q_own.start()

    def send_counts(phase, axis, value):
        size = 2 if axis == "blk_2" else RING
        counts[phase, 0] = value
        for j in range(1, size):
            remote(counts.at[phase, 0], counts.at[phase, size - j], c_sem.at[0, phase], c_sem.at[1, phase],
                   {axis: shifted(at, axis, j)}).start()

    def sum_counts(phase, axis):
        size = 2 if axis == "blk_2" else RING
        got = counts.at[phase, pl.ds(1, size - 1)]
        remote(got, got, c_sem.at[0, phase], c_sem.at[1, phase], {axis: shifted(at, axis, 1)}).wait()
        total = counts[phase, 0]
        for j in range(1, size):
            total = total + counts[phase, j]
        return total

    docs = lax.broadcasted_iota(jnp.int32, (NDOC, seg.shape[1]), 0)
    send_counts(0, "uly", jnp.where(seg[...] < docs, 1, 0))

    for peer in square_peers(at):
        i, j = (peer["blk_0"], peer["uly"])
        remote(q_part(i, j), q_out.at[x * RING + z], q_sem.at[0], q_sem.at[1], peer).start()

    for copy in own:
        copy.wait()
    got = kv.at[0, pl.ds(0, 2 * (RING - 1) * rows)]
    remote(got, got, z_sem.at[0], z_sem.at[1], {"uly": shifted(at, "uly", 1)}).wait()

    streams = (
        (0, 0, FIRST_ROWS, "blk_0", "blk_1"),
        (1, FIRST_ROWS, 2 * UNIT - FIRST_ROWS, "blk_1", "blk_0"),
    )
    order = (0, -1, 1, 2)

    def region(stream, i, j, half=None):
        _, start, size, first, _ = stream
        if half is not None:
            size //= 2
            start += half * size
        return kv.at[block(i, j) if first == "blk_0" else block(j, i), pl.ds(start, size)]

    def ring_copy(stream, what, axis, by, slot):
        return remote(what, what, stream_send.at[stream[0]], stream_recv.at[stream[0], slot], {axis: shifted(at, axis, by)})

    def to_core(what):
        remote(what, what, core_sem.at[0], core_sem.at[1], {"blk_2": 1 - c}).start()

    def spread(stream, axis, slot, pick):
        ring_copy(stream, pick(0), axis, 1, slot).start()
        ring_copy(stream, pick(0), axis, -1, slot + 1).start()

    def relay(stream, axis, slot, pick):
        ring_copy(stream, pick(-1), axis, 1, slot).wait_recv()
        ring_copy(stream, pick(-1, 0), axis, 1, slot + 2).start()
        ring_copy(stream, pick(1), axis, -1, slot + 1).wait_recv()
        ring_copy(stream, pick(1, 1), axis, -1, slot + 3).start()

    def settle(stream, axis, slot, pick):
        ring_copy(stream, pick(2, 0), axis, 1, slot + 2).wait_recv()
        ring_copy(stream, pick(2, 1), axis, -1, slot + 3).wait_recv()

    def along_first(stream):
        return lambda i, half=None: region(stream, i, 0, half)

    def along_second(stream, i):
        return lambda j, half=None: region(stream, i, j, half)

    for s in streams:
        spread(s, s[3], 0, along_first(s))
    for s in streams:
        spread(s, s[4], 4, along_second(s, 0))
    to_core(kv.at[me])
    send_counts(1, "blk_0", sum_counts(0, "uly"))
    for s in streams:
        relay(s, s[3], 0, along_first(s))
        for n in (1, 2):
            spread(s, s[4], 4 + 4 * n, along_second(s, order[n]))
            to_core(region(s, order[n], 0))
    send_counts(2, "blk_1", sum_counts(1, "blk_0"))
    for s in streams:
        relay(s, s[4], 4, along_second(s, 0))
        to_core(region(s, 0, -1))
        to_core(region(s, 0, 1))
    for s in streams:
        settle(s, s[3], 0, along_first(s))
        spread(s, s[4], 16, along_second(s, 2))
        to_core(region(s, 2, 0))
    send_counts(3, "blk_2", sum_counts(2, "blk_1"))
    for n in (1, 2, 3):
        for s in streams:
            settle(s, s[4], 4 * n, along_second(s, order[n - 1]))
            to_core(region(s, order[n - 1], 2))
            relay(s, s[4], 4 + 4 * n, along_second(s, order[n]))
            to_core(region(s, order[n], -1))
            to_core(region(s, order[n], 1))
    count_out[...] = jnp.broadcast_to(jnp.sum(sum_counts(3, "blk_2"), axis=1, keepdims=True), count_out.shape)
    for s in streams:
        settle(s, s[4], 16, along_second(s, 2))
        to_core(region(s, 2, 2))
    for s in streams:
        sent = kv.at[pl.ds(0, 15), pl.ds(s[1], s[2])]
        ring_copy(s, sent, s[3], 1, 0).wait_send()
    half = kv.at[pl.ds(0, 16)]
    remote(half, half, core_sem.at[0], core_sem.at[1], {"blk_2": 1 - c}).wait()
    q_own.wait()
    most = q_out.at[pl.ds(0, RING * RING - 1)]
    remote(most, most, q_sem.at[0], q_sem.at[1], {"uly": shifted(at, "uly", 1)}).wait()


def give_back(o_in, out, own_sem, sem):
    at = coordinates()
    x, z = at["blk_0"], at["uly"]
    piece, width = o_in.shape[1:]
    peers = square_peers(at)
    greet(peers)
    here = out.at[pl.ds(pl.multiple_of(x * piece, piece), piece), pl.ds(pl.multiple_of(z * width, width), width)]
    own = pltpu.make_async_copy(o_in.at[x * RING + z], here, own_sem)
    for peer in peers:
        remote(o_in.at[peer["blk_0"] * RING + peer["uly"]], here, sem.at[0], sem.at[1], peer).start()
    own.start()
    own.wait()
    most = o_in.at[pl.ds(0, RING * RING - 1)]
    remote(most, most, sem.at[0], sem.at[1], peers[0]).wait()


def careful(queries, keys, values, segments):
    rows, wide = queries.shape
    piece, width = rows // RING, wide // RING
    anywhere = pl.BlockSpec(memory_space=pl.ANY)
    vm = pl.BlockSpec(memory_space=pltpu.VMEM)
    q, kv, starts = pl.pallas_call(
        exchange,
        out_shape=(
            jax.ShapeDtypeStruct((RING * RING, piece, width), jnp.bfloat16),
            jax.ShapeDtypeStruct((2 * RING * RING, 2 * UNIT, HEAD_SIZE), jnp.bfloat16),
            jax.ShapeDtypeStruct((NDOC, 128), jnp.int32),
        ),
        in_specs=[vm, anywhere, anywhere, anywhere],
        out_specs=(anywhere, anywhere, vm),
        scratch_shapes=[
            pltpu.VMEM((4, RING, NDOC, rows), jnp.int32),
            pltpu.SemaphoreType.DMA((3,)),
            pltpu.SemaphoreType.DMA((2,)),
            pltpu.SemaphoreType.DMA((2,)),
            pltpu.SemaphoreType.DMA((2, 4)),
            pltpu.SemaphoreType.DMA((2,)),
            pltpu.SemaphoreType.DMA((2, 20)),
            pltpu.SemaphoreType.DMA((2,)),
        ],
        compiler_params=pltpu.CompilerParams(collective_id=1, has_side_effects=True),
        name="exchange",
    )(segments.reshape(1, rows), queries, keys, values)
    out = attention(starts, q, kv)
    return pl.pallas_call(
        give_back,
        out_shape=jax.ShapeDtypeStruct((rows, wide), jnp.bfloat16),
        in_specs=[anywhere],
        out_specs=anywhere,
        scratch_shapes=[pltpu.SemaphoreType.DMA, pltpu.SemaphoreType.DMA((2,))],
        compiler_params=pltpu.CompilerParams(collective_id=2, has_side_effects=True),
        name="give_back",
    )(out)


COLUMN = 2 * UNIT
REACH = 8
CHUNK = 2080
CHUNKS = 4
WAITS = (
    (0, (1, 2), (0, 1, 2), 3),
    (2, (3,), (), 0),
    (3, (8,), (), 3),
    (4, (), (3, 4), 0),
    (6, (5, 6), (), 0),
    (7, (7,), (), 0),
    (8, (), (5, 6), 0),
    (9, (), (7, 8), 0),
)
LIMIT = 100.0


def ring_attend(seg, q_in, k_in, v_in, out, stats_out, kv, qbuf, obuf, qv, kv_own, qcat, acc, stats,
                local_sem, bar_z, q_sem, s_sem, send_sem, recv_sem, core_send, core_recv, o_sem):
    D = HEAD_SIZE
    x, y, c, z = (lax.axis_index(a) for a in AXES)
    column = x * RING + y
    rows = q_in.shape[0]
    width = q_in.shape[1] // RING

    def peer(axis, by):
        size = 2 if axis == "blk_2" else RING
        return {axis: lax.rem(lax.axis_index(axis) + by, size)}

    def group(phase):
        if phase == 0:
            return [peer("uly", j) for j in range(1, RING)]
        if phase == 2:
            return [peer("blk_0", j) for j in range(1, RING)]
        return [{**peer("blk_1", j % RING), **peer("blk_2", j // RING)} for j in range(1, 2 * RING)]

    greet(group(0) + group(1) + group(2))

    def place(d, core):
        return pl.ds(pl.multiple_of((REACH - d) * COLUMN + core * UNIT, UNIT), UNIT)

    mine = pl.ds(pl.multiple_of(REACH * COLUMN + c * UNIT + z * rows, rows), rows)

    def head(ref, h, size):
        return ref.at[:, pl.ds(pl.multiple_of(h * size, size), size)]

    for j in (1, 3, 2):
        to = peer("uly", j)
        remote(head(k_in, to["uly"], D), kv.at[0, mine], bar_z.at[0], bar_z.at[1], to).start()
        remote(head(v_in, to["uly"], D), kv.at[1, mine], bar_z.at[0], bar_z.at[1], to).start()
    own = [
        pltpu.make_async_copy(head(k_in, z, D), kv.at[0, mine], local_sem.at[0]),
        pltpu.make_async_copy(head(v_in, z, D), kv.at[1, mine], local_sem.at[1]),
        pltpu.make_async_copy(head(q_in, z, width), qbuf.at[0], local_sem.at[2]),
        pltpu.make_async_copy(q_in, qv, local_sem.at[3]),
        pltpu.make_async_copy(k_in, kv_own, local_sem.at[4]),
    ]
    for copy in own:
        copy.start()
    @pl.loop(1, REACH + 1)
    def _(d):
        @pl.when(column < d)
        def _():
            at = pl.ds(pl.multiple_of((REACH - d) * COLUMN, COLUMN), COLUMN)
            kv[0, at] = jnp.zeros((COLUMN, D), kv.dtype)
            kv[1, at] = jnp.zeros((COLUMN, D), kv.dtype)

    own[3].wait()
    own[4].wait()

    def longest(ref):
        most = jnp.zeros((rows, 1), jnp.float32)
        for h in range(ref.shape[1] // D):
            a = ref[:, h * D:(h + 1) * D].astype(jnp.float32)
            most = jnp.maximum(most, jnp.sum(a * a, axis=1, keepdims=True))
        return jnp.broadcast_to(jnp.max(most, axis=0, keepdims=True), (1, rows))

    kind = lax.broadcasted_iota(jnp.int32, (2 * NDOC, rows), 0)
    before = jnp.where(seg[...] < kind, 1.0, 0.0)
    before = jnp.where(kind == NDOC, longest(qv), jnp.where(kind > NDOC, longest(kv_own), before))

    def send_stats(phase, value):
        stats[phase, 0] = value
        to = group(phase)
        for n, target in enumerate(to):
            slot = (n + 1) % RING + (n + 1) // RING * RING
            slot = (RING - slot % RING) % RING + slot // RING * RING
            remote(stats.at[phase, 0], stats.at[phase, slot], s_sem.at[0, phase], s_sem.at[1, phase], target).start()

    def sum_stats(phase):
        size = len(group(phase)) + 1
        got = stats.at[phase, pl.ds(1, size - 1)]
        remote(got, got, s_sem.at[0, phase], s_sem.at[1, phase], group(phase)[0]).wait()
        total = stats[phase, 0]
        for j in range(1, size):
            other = stats[phase, j]
            total = jnp.where(kind < NDOC, total + other, jnp.maximum(total, other))
        return total

    send_stats(0, before)
    own[0].wait()
    own[1].wait()
    got = kv.at[0, pl.ds(0, 2 * (RING - 1) * rows)]
    remote(got, got, bar_z.at[0], bar_z.at[1], peer("uly", 1)).wait()
    for j in (1, 3, 2):
        to = peer("uly", j)
        remote(head(q_in, to["uly"], width), qbuf.at[RING - j], q_sem.at[0, j], q_sem.at[1, RING - j], to).start()


    def move(n, from_d, to_d, to):
        return remote(kv.at[:, place(from_d, c)], kv.at[:, place(to_d, c)], send_sem.at[n], recv_sem.at[to_d], to)

    moves = []

    def start_if(able, *what):
        moves.append((able, what))

        @pl.when(able)
        def _():
            move(*what).start()

    def received(d):
        @pl.when(column >= d)
        def _():
            move(0, d, d, {"blk_1": y}).wait_recv()
            to_core(d).start()

    def to_core(d):
        what = kv.at[:, place(d, c)]
        return remote(what, what, core_send.at[d], core_recv.at[d], {"blk_2": 1 - c})

    def from_core(d):
        @pl.when(column >= d)
        def _():
            to_core(d).wait_recv()

    later = []

    def start_later(able, *what):
        moves.append((able, what))
        later.append((able, what))

    def flush(count):
        for _ in range(count):
            able, what = later.pop(0)

            @pl.when(able)
            def _(what=what):
                move(*what).start()

    send_stats(1, sum_stats(0))
    for j in (1, 2, 3):
        start_if(y + j < RING, 1 + j, 0, j, peer("blk_1", j))
    start_if(x < 3, 0, 0, 4, peer("blk_0", 1))
    to_core(0).start()
    send_stats(2, sum_stats(1))
    received(4)
    start_if((x >= 1) & (x < 3), 1, 4, 8, peer("blk_0", 1))
    for j in (1, 2, 3):
        start_if((x >= 1) & (y >= j), 4 + j, 4, 4 - j, peer("blk_1", RING - j))
    for j in (1, 2, 3):
        start_later((x >= 1) & (y + j < RING), 10 + j, 4, 4 + j, peer("blk_1", j))
    for j in (1, 2, 3):
        start_later((x >= 2) & (y >= j), 7 + j, 8, 8 - j, peer("blk_1", RING - j))
    final = sum_stats(2)
    reach = final[NDOC:NDOC + 1] * final[NDOC + 1:NDOC + 2] * SCALE2 ** 2
    stats_out[0] = jnp.min(jnp.where(reach < LIMIT ** 2, 1, 0))
    starts = jnp.sum(final[:NDOC], axis=1, keepdims=True).astype(jnp.int32)
    starts = jnp.broadcast_to(starts, (NDOC, rows))
    own[2].wait()

    @pl.loop(0, RING * CHUNKS)
    def _(n):
        early = n < 2 * RING
        last = (n - 2 * RING) // 2
        turn = jnp.where(early, n % RING, jnp.where(last == 0, 2, jnp.where(last == RING - 1, 0, 2 * last - 1)))
        chunk = jnp.where(early, n // RING, 2 + n % 2)
        to = lax.rem(z + turn, RING)

        for at_step, arrivals, crossed, count in WAITS:
            @pl.when(n == at_step)
            def _(arrivals=arrivals, crossed=crossed, count=count):
                for d in arrivals:
                    received(d)
                for d in crossed:
                    from_core(d)
                flush(count)

        @pl.when(chunk == 0)
        def _():
            @pl.when(turn > 0)
            def _():
                remote(qbuf.at[turn], qbuf.at[turn], q_sem.at[0, turn], q_sem.at[1, turn], {"uly": to}).wait_recv()

            for g in range(GROUP):
                q = qbuf[turn, :, g * D:(g + 1) * D].astype(jnp.float32) * SCALE2
                high = q.astype(jnp.bfloat16)
                at = slice(g * rows, (g + 1) * rows)
                qcat[turn, at, :D] = high
                qcat[turn, at, D:] = (q - high.astype(jnp.float32)).astype(jnp.bfloat16)
            acc[turn] = jnp.zeros(acc.shape[1:], acc.dtype)

        qpos = column * COLUMN + c * UNIT + to * rows + lax.broadcasted_iota(jnp.int32, (1, rows), 1)
        qlow = jnp.zeros_like(qpos)
        for d in range(1, NDOC):
            qlow = jnp.where(starts[d:d + 1] <= qpos, jnp.maximum(qlow, starts[d:d + 1]), qlow)
        first = c * UNIT + to * rows + (CHUNKS - 1 - chunk) * CHUNK
        at = pl.ds(pl.multiple_of(first, 32), CHUNK)
        kpos = (column - REACH) * COLUMN + first + lax.broadcasted_iota(jnp.int32, (CHUNK, rows), 0)
        allowed = (kpos <= qpos) & (kpos >= qlow)
        k = kv[0, at]
        v = kv[1, at]
        kk = jnp.concatenate([k, k], axis=1)
        vv = jnp.concatenate([v, jnp.ones((CHUNK, ONES), v.dtype)], axis=1)
        p = jnp.exp2(contract(kk, qcat[turn], 1, 1))
        p = jnp.concatenate([jnp.where(allowed, p[:, g * rows:(g + 1) * rows], 0.0) for g in range(GROUP)], axis=1)
        acc[turn] += contract(vv, p.astype(jnp.bfloat16), 0, 0)

        @pl.when(chunk == CHUNKS - 1)
        def _():
            for g in range(GROUP):
                a = slice(g * rows, (g + 1) * rows)
                o = acc[turn, :D, a] / acc[turn, D:D + 1, a]
                obuf[turn, :, g * D:(g + 1) * D] = o.T.astype(jnp.bfloat16)

            @pl.when(turn == 0)
            def _():
                pltpu.make_async_copy(obuf.at[0], head(out, z, width), local_sem.at[5]).start()

            @pl.when(turn > 0)
            def _():
                remote(obuf.at[turn], head(out, z, width), o_sem.at[0], o_sem.at[1], {"uly": to}).start()

    for able, what in moves:
        @pl.when(able)
        def _(what=what):
            move(*what).wait_send()
    for d in range(REACH + 1):
        @pl.when(column >= d)
        def _(d=d):
            to_core(d).wait_send()
    for j in range(1, RING):
        remote(qbuf.at[j], qbuf.at[j], q_sem.at[0, j], q_sem.at[1, j], peer("uly", j)).wait_send()
    pltpu.make_async_copy(obuf.at[0], head(out, z, width), local_sem.at[5]).wait()
    got = obuf.at[pl.ds(1, RING - 1)]
    remote(got, got, o_sem.at[0], o_sem.at[1], peer("uly", 1)).wait()


def local(queries, keys, values, segments):
    rows, wide = queries.shape
    width = wide // RING
    M = GROUP * rows
    anywhere = pl.BlockSpec(memory_space=pl.ANY)
    vm = pl.BlockSpec(memory_space=pltpu.VMEM)
    out, stats = pl.pallas_call(
        ring_attend,
        out_shape=(
            jax.ShapeDtypeStruct((rows, wide), jnp.bfloat16),
            jax.ShapeDtypeStruct((1,), jnp.int32),
        ),
        in_specs=[vm, anywhere, anywhere, anywhere],
        out_specs=(anywhere, pl.BlockSpec(memory_space=pltpu.SMEM)),
        scratch_shapes=[
            pltpu.VMEM((2, (REACH + 1) * COLUMN, HEAD_SIZE), jnp.bfloat16),
            pltpu.VMEM((RING, rows, width), jnp.bfloat16),
            pltpu.VMEM((RING, rows, width), jnp.bfloat16),
            pltpu.VMEM((rows, wide), jnp.bfloat16),
            pltpu.VMEM((rows, RING * HEAD_SIZE), jnp.bfloat16),
            pltpu.VMEM((RING, M, 2 * HEAD_SIZE), jnp.bfloat16),
            pltpu.VMEM((RING, HEAD_SIZE + ONES, M), jnp.float32),
            pltpu.VMEM((3, 2 * RING, 2 * NDOC, rows), jnp.float32),
            pltpu.SemaphoreType.DMA((6,)),
            pltpu.SemaphoreType.DMA((2,)),
            pltpu.SemaphoreType.DMA((2, RING)),
            pltpu.SemaphoreType.DMA((2, 4)),
            pltpu.SemaphoreType.DMA((14,)),
            pltpu.SemaphoreType.DMA((REACH + 1,)),
            pltpu.SemaphoreType.DMA((REACH + 1,)),
            pltpu.SemaphoreType.DMA((REACH + 1,)),
            pltpu.SemaphoreType.DMA((2,)),
        ],
        compiler_params=pltpu.CompilerParams(collective_id=0, has_side_effects=True, vmem_limit_bytes=56 << 20),
        name="ring_attend",
    )(segments.reshape(1, rows), queries, keys, values)
    return lax.cond(stats[0] == 1, lambda *_: out, careful, queries, keys, values, segments)


def solution(mesh):
    split = Mesh(mesh.devices.reshape(4, 4, 2, mesh.shape["uly"]), AXES)
    return jax.shard_map(
        local,
        mesh=split,
        in_specs=(P(AXES, None), P(AXES, None), P(AXES, None), P(AXES)),
        out_specs=P(AXES, None),
        check_vma=False,
    )
```

```python
import functools
import jax, jax.numpy as jnp
from jax import lax
from jax.experimental import pallas as pl
from jax.experimental.pallas import tpu as pltpu
from jax.sharding import Mesh
from jax.sharding import PartitionSpec as P

HEAD_SIZE = 128
NDOC = 8
GROUP = 8
SCALE2 = 1.4426950408889634 * HEAD_SIZE ** -0.5
ONES = 16
UNIT = 512
BIG = 2048


def doc_start(info, pos):
    low = jnp.zeros_like(pos)
    for d in range(1, NDOC):
        low = jnp.where(info[d, 0] <= pos, jnp.maximum(low, info[d, 0]), low)
    return low


def contract(a, b, da, db):
    return lax.dot_general(a, b, (((da,), (db,)), ((), ())), preferred_element_type=jnp.float32)


def attend(place, info, q_ref, kv, o_ref, kbuf, vbuf, qcat, acc, top, sems):
    D = HEAD_SIZE
    piece = q_ref.shape[1]
    tiles = pieces = RING
    rows = pieces * piece
    M = GROUP * rows
    blocks = kbuf.shape[0] // tiles
    part = blocks * UNIT
    offset, stripe = place()
    shard = UNIT // pieces

    def loads(t):
        at = pl.ds(t * blocks, blocks)
        return (
            pltpu.make_async_copy(kv.at[at, pl.ds(0, UNIT)], kbuf.at[at], sems.at[0, t]),
            pltpu.make_async_copy(kv.at[at, pl.ds(UNIT, UNIT)], vbuf.at[at], sems.at[1, t]),
        )

    for t in range(tiles):
        for c in loads(t):
            c.start()

    @pl.loop(0, tiles)
    def _(t):
        base = offset + t * part
        first = base + stripe
        last = first + (pieces - 1) * shard + piece - 1
        for c in loads(t):
            c.wait()
        low = doc_start(info, first) // UNIT
        diag = base // UNIT
        lane = lax.broadcasted_iota(jnp.int32, (1, rows), 1)
        qpos = first + (lane // piece) * shard + lane % piece
        qlow = doc_start(info, qpos)

        for g in range(GROUP):
            q = q_ref[pl.ds(t * pieces, pieces), :, g * D:(g + 1) * D].reshape(rows, D).astype(jnp.float32) * SCALE2
            high = q.astype(jnp.bfloat16)
            at = slice(g * rows, (g + 1) * rows)
            qcat[at, :D] = high
            qcat[at, D:] = (q - high.astype(jnp.float32)).astype(jnp.bfloat16)
        acc[...] = jnp.zeros_like(acc)

        def allowed(at, size):
            kpos = at + lax.broadcasted_iota(jnp.int32, (size, rows), 0)
            return (kpos <= qpos) & (kpos >= qlow)

        def masked(p, m):
            return jnp.concatenate(
                [jnp.where(m, p[:, g * rows:(g + 1) * rows], 0.0) for g in range(p.shape[1] // rows)], axis=1)

        def step(at, size):
            k = kbuf[pl.ds(at, size // UNIT)].reshape(size, D)
            v = vbuf[pl.ds(at, size // UNIT)].reshape(size, D)
            kk = jnp.concatenate([k, k], axis=1)
            vv = jnp.concatenate([v, jnp.ones((size, ONES), v.dtype)], axis=1)
            p = masked(jnp.exp2(contract(kk, qcat[...], 1, 1)), allowed(at * UNIT, size))
            acc[...] += contract(vv, p.astype(jnp.bfloat16), 0, 0)

        units = diag + 1 - low
        per = BIG // UNIT
        big = units // per

        @pl.loop(0, big)
        def _(n):
            step(low + n * per, BIG)

        size = BIG // 2
        done = low + big * per
        while size >= UNIT:
            some = (units // (size // UNIT)) % 2

            @pl.when(some == 1)
            def _(done=done, size=size):
                step(done, size)

            done = done + some * (size // UNIT)
            size //= 2

        total = acc[D:D + 8, :]
        good = jnp.min(jnp.where((total > 2.0 ** -60) & (total < 2.0 ** 118), 1.0, 0.0))

        @pl.when(good < 0.5)
        def _():
            top[...] = jnp.full_like(top, -1e30)
            acc[...] = jnp.zeros_like(acc)

            def scores(n, g):
                q = q_ref[pl.ds(t * pieces, pieces), :, pl.ds(pl.multiple_of(g * D, D), D)].reshape(rows, D)
                m = allowed(n * UNIT, UNIT)
                return jnp.where(m, contract(kbuf[n], q, 1, 1) * SCALE2, -1e30), m

            @pl.loop(low, diag + 1)
            def _(n):
                @pl.loop(0, GROUP)
                def _(g):
                    at = pl.ds(pl.multiple_of(g * rows, rows), rows)
                    s, _ = scores(n, g)
                    top[:, at] = jnp.maximum(top[:, at], jnp.max(s, axis=0, keepdims=True))

            @pl.loop(low, diag + 1)
            def _(n):
                v = vbuf[n]
                vv = jnp.concatenate([v, jnp.ones((UNIT, ONES), v.dtype)], axis=1)

                @pl.loop(0, GROUP)
                def _(g):
                    at = pl.ds(pl.multiple_of(g * rows, rows), rows)
                    s, m = scores(n, g)
                    p = jnp.where(m, jnp.exp2(s - top[:1, at]), 0.0)
                    acc[:, at] += contract(vv, p.astype(jnp.bfloat16), 0, 0)

        for g in range(GROUP):
            at = slice(g * rows, (g + 1) * rows)
            out = acc[:D, at] / acc[D:D + 1, at]
            o_ref[pl.ds(t * pieces, pieces), :, g * D:(g + 1) * D] = out.T.astype(jnp.bfloat16).reshape(pieces, piece, D)


def place():
    return (
        lax.axis_index(("blk_1", "blk_2")) * UNIT,
        lax.axis_index("blk_0") * (UNIT // RING // RING),
    )


def attention(starts, q, kv, place=place):
    M = GROUP * RING * q.shape[1]
    vm = pl.BlockSpec(memory_space=pltpu.VMEM)
    half = (kv.shape[0], UNIT, HEAD_SIZE)
    return pl.pallas_call(
        functools.partial(attend, place),
        out_shape=jax.ShapeDtypeStruct(q.shape, jnp.bfloat16),
        in_specs=[pl.BlockSpec(memory_space=pltpu.SMEM), vm, pl.BlockSpec(memory_space=pl.ANY)],
        out_specs=vm,
        scratch_shapes=[
            pltpu.VMEM(half, jnp.bfloat16),
            pltpu.VMEM(half, jnp.bfloat16),
            pltpu.VMEM((M, 2 * HEAD_SIZE), jnp.bfloat16),
            pltpu.VMEM((HEAD_SIZE + ONES, M), jnp.float32),
            pltpu.VMEM((8, M), jnp.float32),
            pltpu.SemaphoreType.DMA((2, RING)),
        ],
        compiler_params=pltpu.CompilerParams(vmem_limit_bytes=56 << 20),
        name="attend",
    )(starts, q, kv)


AXES = ("blk_0", "blk_1", "blk_2", "uly")
RING = 4
K_ROWS = UNIT
FIRST_ROWS = 768


def coordinates():
    return {axis: lax.axis_index(axis) for axis in AXES}


def shifted(at, axis, by):
    size = 2 if axis == "blk_2" else RING
    return lax.rem(at[axis] + (by + size), size)


def greet(peers):
    barrier = pltpu.get_barrier_semaphore()
    for peer in peers:
        pl.semaphore_signal(barrier, inc=1, device_id=peer, device_id_type=pl.DeviceIdType.MESH)
    pl.semaphore_wait(barrier, len(peers))


def remote(src, dst, send, recv, peer):
    return pltpu.make_async_remote_copy(
        src_ref=src, dst_ref=dst, send_sem=send, recv_sem=recv, device_id=peer,
        device_id_type=pl.DeviceIdType.MESH)


def square_peers(at):
    return [
        {"blk_0": shifted(at, "blk_0", i), "uly": shifted(at, "uly", j)}
        for i in range(RING) for j in range(RING) if i or j
    ]


def exchange(seg, q_in, k_in, v_in, q_out, kv, count_out, counts, own_sem, q_sem, z_sem, c_sem, stream_send, stream_recv, core_sem):
    D = HEAD_SIZE
    at = coordinates()
    x, y, c, z = (at[a] for a in AXES)
    rows = q_in.shape[0]
    piece = rows // RING
    width = q_in.shape[1] // RING
    greet(square_peers(at) + [{"blk_1": shifted(at, "blk_1", j)} for j in range(1, RING)] + [{"blk_2": 1 - c}])

    def block(i, j):
        return (shifted(at, "blk_0", i) * RING + shifted(at, "blk_1", j)) * 2 + c

    me = block(0, 0)
    mine = pl.ds(pl.multiple_of(z * rows, rows), rows)
    low = pl.ds(pl.multiple_of(UNIT + z * rows, rows), rows)

    def head(ref, h):
        return ref.at[:, pl.ds(pl.multiple_of(h * D, D), D)]

    own = [
        pltpu.make_async_copy(head(k_in, z), kv.at[me, mine], own_sem.at[0]),
        pltpu.make_async_copy(head(v_in, z), kv.at[me, low], own_sem.at[1]),
    ]
    for copy in own:
        copy.start()
    for j in range(1, RING):
        to = shifted(at, "uly", j)
        remote(head(k_in, to), kv.at[me, mine], z_sem.at[0], z_sem.at[1], {"uly": to}).start()
        remote(head(v_in, to), kv.at[me, low], z_sem.at[0], z_sem.at[1], {"uly": to}).start()

    def q_part(i, j):
        return q_in.at[pl.ds(pl.multiple_of(i * piece, piece), piece), pl.ds(pl.multiple_of(j * width, width), width)]

    q_own = pltpu.make_async_copy(q_part(x, z), q_out.at[x * RING + z], own_sem.at[2])
    q_own.start()

    def send_counts(phase, axis, value):
        size = 2 if axis == "blk_2" else RING
        counts[phase, 0] = value
        for j in range(1, size):
            remote(counts.at[phase, 0], counts.at[phase, size - j], c_sem.at[0, phase], c_sem.at[1, phase],
                   {axis: shifted(at, axis, j)}).start()

    def sum_counts(phase, axis):
        size = 2 if axis == "blk_2" else RING
        got = counts.at[phase, pl.ds(1, size - 1)]
        remote(got, got, c_sem.at[0, phase], c_sem.at[1, phase], {axis: shifted(at, axis, 1)}).wait()
        total = counts[phase, 0]
        for j in range(1, size):
            total = total + counts[phase, j]
        return total

    docs = lax.broadcasted_iota(jnp.int32, (NDOC, seg.shape[1]), 0)
    send_counts(0, "uly", jnp.where(seg[...] < docs, 1, 0))

    for peer in square_peers(at):
        i, j = (peer["blk_0"], peer["uly"])
        remote(q_part(i, j), q_out.at[x * RING + z], q_sem.at[0], q_sem.at[1], peer).start()

    for copy in own:
        copy.wait()
    got = kv.at[0, pl.ds(0, 2 * (RING - 1) * rows)]
    remote(got, got, z_sem.at[0], z_sem.at[1], {"uly": shifted(at, "uly", 1)}).wait()

    streams = (
        (0, 0, FIRST_ROWS, "blk_0", "blk_1"),
        (1, FIRST_ROWS, 2 * UNIT - FIRST_ROWS, "blk_1", "blk_0"),
    )
    order = (0, -1, 1, 2)

    def region(stream, i, j, half=None):
        _, start, size, first, _ = stream
        if half is not None:
            size //= 2
            start += half * size
        return kv.at[block(i, j) if first == "blk_0" else block(j, i), pl.ds(start, size)]

    def ring_copy(stream, what, axis, by, slot):
        return remote(what, what, stream_send.at[stream[0]], stream_recv.at[stream[0], slot], {axis: shifted(at, axis, by)})

    def to_core(what):
        remote(what, what, core_sem.at[0], core_sem.at[1], {"blk_2": 1 - c}).start()

    def spread(stream, axis, slot, pick):
        ring_copy(stream, pick(0), axis, 1, slot).start()
        ring_copy(stream, pick(0), axis, -1, slot + 1).start()

    def relay(stream, axis, slot, pick):
        ring_copy(stream, pick(-1), axis, 1, slot).wait_recv()
        ring_copy(stream, pick(-1, 0), axis, 1, slot + 2).start()
        ring_copy(stream, pick(1), axis, -1, slot + 1).wait_recv()
        ring_copy(stream, pick(1, 1), axis, -1, slot + 3).start()

    def settle(stream, axis, slot, pick):
        ring_copy(stream, pick(2, 0), axis, 1, slot + 2).wait_recv()
        ring_copy(stream, pick(2, 1), axis, -1, slot + 3).wait_recv()

    def along_first(stream):
        return lambda i, half=None: region(stream, i, 0, half)

    def along_second(stream, i):
        return lambda j, half=None: region(stream, i, j, half)

    for s in streams:
        spread(s, s[3], 0, along_first(s))
    for s in streams:
        spread(s, s[4], 4, along_second(s, 0))
    to_core(kv.at[me])
    send_counts(1, "blk_0", sum_counts(0, "uly"))
    for s in streams:
        relay(s, s[3], 0, along_first(s))
        for n in (1, 2):
            spread(s, s[4], 4 + 4 * n, along_second(s, order[n]))
            to_core(region(s, order[n], 0))
    send_counts(2, "blk_1", sum_counts(1, "blk_0"))
    for s in streams:
        relay(s, s[4], 4, along_second(s, 0))
        to_core(region(s, 0, -1))
        to_core(region(s, 0, 1))
    for s in streams:
        settle(s, s[3], 0, along_first(s))
        spread(s, s[4], 16, along_second(s, 2))
        to_core(region(s, 2, 0))
    send_counts(3, "blk_2", sum_counts(2, "blk_1"))
    for n in (1, 2, 3):
        for s in streams:
            settle(s, s[4], 4 * n, along_second(s, order[n - 1]))
            to_core(region(s, order[n - 1], 2))
            relay(s, s[4], 4 + 4 * n, along_second(s, order[n]))
            to_core(region(s, order[n], -1))
            to_core(region(s, order[n], 1))
    count_out[...] = jnp.broadcast_to(jnp.sum(sum_counts(3, "blk_2"), axis=1, keepdims=True), count_out.shape)
    for s in streams:
        settle(s, s[4], 16, along_second(s, 2))
        to_core(region(s, 2, 2))
    for s in streams:
        sent = kv.at[pl.ds(0, 15), pl.ds(s[1], s[2])]
        ring_copy(s, sent, s[3], 1, 0).wait_send()
    half = kv.at[pl.ds(0, 16)]
    remote(half, half, core_sem.at[0], core_sem.at[1], {"blk_2": 1 - c}).wait()
    q_own.wait()
    most = q_out.at[pl.ds(0, RING * RING - 1)]
    remote(most, most, q_sem.at[0], q_sem.at[1], {"uly": shifted(at, "uly", 1)}).wait()


def give_back(o_in, out, own_sem, sem):
    at = coordinates()
    x, z = at["blk_0"], at["uly"]
    piece, width = o_in.shape[1:]
    peers = square_peers(at)
    greet(peers)
    here = out.at[pl.ds(pl.multiple_of(x * piece, piece), piece), pl.ds(pl.multiple_of(z * width, width), width)]
    own = pltpu.make_async_copy(o_in.at[x * RING + z], here, own_sem)
    for peer in peers:
        remote(o_in.at[peer["blk_0"] * RING + peer["uly"]], here, sem.at[0], sem.at[1], peer).start()
    own.start()
    own.wait()
    most = o_in.at[pl.ds(0, RING * RING - 1)]
    remote(most, most, sem.at[0], sem.at[1], peers[0]).wait()


def careful(queries, keys, values, segments):
    rows, wide = queries.shape
    piece, width = rows // RING, wide // RING
    anywhere = pl.BlockSpec(memory_space=pl.ANY)
    vm = pl.BlockSpec(memory_space=pltpu.VMEM)
    q, kv, starts = pl.pallas_call(
        exchange,
        out_shape=(
            jax.ShapeDtypeStruct((RING * RING, piece, width), jnp.bfloat16),
            jax.ShapeDtypeStruct((2 * RING * RING, 2 * UNIT, HEAD_SIZE), jnp.bfloat16),
            jax.ShapeDtypeStruct((NDOC, 128), jnp.int32),
        ),
        in_specs=[vm, anywhere, anywhere, anywhere],
        out_specs=(anywhere, anywhere, vm),
        scratch_shapes=[
            pltpu.VMEM((4, RING, NDOC, rows), jnp.int32),
            pltpu.SemaphoreType.DMA((3,)),
            pltpu.SemaphoreType.DMA((2,)),
            pltpu.SemaphoreType.DMA((2,)),
            pltpu.SemaphoreType.DMA((2, 4)),
            pltpu.SemaphoreType.DMA((2,)),
            pltpu.SemaphoreType.DMA((2, 20)),
            pltpu.SemaphoreType.DMA((2,)),
        ],
        compiler_params=pltpu.CompilerParams(collective_id=1, has_side_effects=True),
        name="exchange",
    )(segments.reshape(1, rows), queries, keys, values)
    out = attention(starts, q, kv)
    return pl.pallas_call(
        give_back,
        out_shape=jax.ShapeDtypeStruct((rows, wide), jnp.bfloat16),
        in_specs=[anywhere],
        out_specs=anywhere,
        scratch_shapes=[pltpu.SemaphoreType.DMA, pltpu.SemaphoreType.DMA((2,))],
        compiler_params=pltpu.CompilerParams(collective_id=2, has_side_effects=True),
        name="give_back",
    )(out)


COLUMN = 2 * UNIT
REACH = 8
CHUNK = 2080
CHUNKS = 4
WAITS = (
    (0, (1, 2), (0, 1, 2), 3),
    (2, (3,), (), 0),
    (3, (8,), (), 3),
    (4, (), (3, 4), 0),
    (6, (5, 6), (), 0),
    (7, (7,), (), 0),
    (8, (), (5, 6), 0),
    (9, (), (7, 8), 0),
)
LIMIT = 100.0


def ring_attend(seg, q_in, k_in, v_in, out, stats_out, kv, qbuf, obuf, qv, kv_own, qcat, acc, stats,
                local_sem, bar_z, q_sem, s_sem, send_sem, recv_sem, core_send, core_recv, o_sem):
    D = HEAD_SIZE
    x, y, c, z = (lax.axis_index(a) for a in AXES)
    column = x * RING + y
    rows = q_in.shape[0]
    width = q_in.shape[1] // RING

    def peer(axis, by):
        size = 2 if axis == "blk_2" else RING
        return {axis: lax.rem(lax.axis_index(axis) + by, size)}

    def group(phase):
        if phase == 0:
            return [peer("uly", j) for j in range(1, RING)]
        if phase == 2:
            return [peer("blk_0", j) for j in range(1, RING)]
        return [{**peer("blk_1", j % RING), **peer("blk_2", j // RING)} for j in range(1, 2 * RING)]

    greet(group(0) + group(1) + group(2))

    def place(d, core):
        return pl.ds(pl.multiple_of((REACH - d) * COLUMN + core * UNIT, UNIT), UNIT)

    mine = pl.ds(pl.multiple_of(REACH * COLUMN + c * UNIT + z * rows, rows), rows)

    def head(ref, h, size):
        return ref.at[:, pl.ds(pl.multiple_of(h * size, size), size)]

    for j in (1, 3, 2):
        to = peer("uly", j)
        remote(head(k_in, to["uly"], D), kv.at[0, mine], bar_z.at[0], bar_z.at[1], to).start()
        remote(head(v_in, to["uly"], D), kv.at[1, mine], bar_z.at[0], bar_z.at[1], to).start()
    own = [
        pltpu.make_async_copy(head(k_in, z, D), kv.at[0, mine], local_sem.at[0]),
        pltpu.make_async_copy(head(v_in, z, D), kv.at[1, mine], local_sem.at[1]),
        pltpu.make_async_copy(head(q_in, z, width), qbuf.at[0], local_sem.at[2]),
        pltpu.make_async_copy(q_in, qv, local_sem.at[3]),
        pltpu.make_async_copy(k_in, kv_own, local_sem.at[4]),
    ]
    for copy in own:
        copy.start()
    @pl.loop(1, REACH + 1)
    def _(d):
        @pl.when(column < d)
        def _():
            at = pl.ds(pl.multiple_of((REACH - d) * COLUMN, COLUMN), COLUMN)
            kv[0, at] = jnp.zeros((COLUMN, D), kv.dtype)
            kv[1, at] = jnp.zeros((COLUMN, D), kv.dtype)

    own[3].wait()
    own[4].wait()

    def longest(ref):
        most = jnp.zeros((rows, 1), jnp.float32)
        for h in range(ref.shape[1] // D):
            a = ref[:, h * D:(h + 1) * D].astype(jnp.float32)
            most = jnp.maximum(most, jnp.sum(a * a, axis=1, keepdims=True))
        return jnp.broadcast_to(jnp.max(most, axis=0, keepdims=True), (1, rows))

    kind = lax.broadcasted_iota(jnp.int32, (2 * NDOC, rows), 0)
    before = jnp.where(seg[...] < kind, 1.0, 0.0)
    before = jnp.where(kind == NDOC, longest(qv), jnp.where(kind > NDOC, longest(kv_own), before))

    def send_stats(phase, value):
        stats[phase, 0] = value
        to = group(phase)
        for n, target in enumerate(to):
            slot = (n + 1) % RING + (n + 1) // RING * RING
            slot = (RING - slot % RING) % RING + slot // RING * RING
            remote(stats.at[phase, 0], stats.at[phase, slot], s_sem.at[0, phase], s_sem.at[1, phase], target).start()

    def sum_stats(phase):
        size = len(group(phase)) + 1
        got = stats.at[phase, pl.ds(1, size - 1)]
        remote(got, got, s_sem.at[0, phase], s_sem.at[1, phase], group(phase)[0]).wait()
        total = stats[phase, 0]
        for j in range(1, size):
            other = stats[phase, j]
            total = jnp.where(kind < NDOC, total + other, jnp.maximum(total, other))
        return total

    send_stats(0, before)
    own[0].wait()
    own[1].wait()
    got = kv.at[0, pl.ds(0, 2 * (RING - 1) * rows)]
    remote(got, got, bar_z.at[0], bar_z.at[1], peer("uly", 1)).wait()
    for j in (1, 3, 2):
        to = peer("uly", j)
        remote(head(q_in, to["uly"], width), qbuf.at[RING - j], q_sem.at[0, j], q_sem.at[1, RING - j], to).start()


    def move(n, from_d, to_d, to):
        return remote(kv.at[:, place(from_d, c)], kv.at[:, place(to_d, c)], send_sem.at[n], recv_sem.at[to_d], to)

    moves = []

    def start_if(able, *what):
        moves.append((able, what))

        @pl.when(able)
        def _():
            move(*what).start()

    def received(d):
        @pl.when(column >= d)
        def _():
            move(0, d, d, {"blk_1": y}).wait_recv()
            to_core(d).start()

    def to_core(d):
        what = kv.at[:, place(d, c)]
        return remote(what, what, core_send.at[d], core_recv.at[d], {"blk_2": 1 - c})

    def from_core(d):
        @pl.when(column >= d)
        def _():
            to_core(d).wait_recv()

    later = []

    def start_later(able, *what):
        moves.append((able, what))
        later.append((able, what))

    def flush(count):
        for _ in range(count):
            able, what = later.pop(0)

            @pl.when(able)
            def _(what=what):
                move(*what).start()

    send_stats(1, sum_stats(0))
    for j in (1, 2, 3):
        start_if(y + j < RING, 1 + j, 0, j, peer("blk_1", j))
    start_if(x < 3, 0, 0, 4, peer("blk_0", 1))
    to_core(0).start()
    send_stats(2, sum_stats(1))
    received(4)
    start_if((x >= 1) & (x < 3), 1, 4, 8, peer("blk_0", 1))
    for j in (1, 2, 3):
        start_if((x >= 1) & (y >= j), 4 + j, 4, 4 - j, peer("blk_1", RING - j))
    for j in (1, 2, 3):
        start_later((x >= 1) & (y + j < RING), 10 + j, 4, 4 + j, peer("blk_1", j))
    for j in (1, 2, 3):
        start_later((x >= 2) & (y >= j), 7 + j, 8, 8 - j, peer("blk_1", RING - j))
    final = sum_stats(2)
    reach = final[NDOC:NDOC + 1] * final[NDOC + 1:NDOC + 2] * SCALE2 ** 2
    stats_out[0] = jnp.min(jnp.where(reach < LIMIT ** 2, 1, 0))
    starts = jnp.sum(final[:NDOC], axis=1, keepdims=True).astype(jnp.int32)
    starts = jnp.broadcast_to(starts, (NDOC, rows))
    own[2].wait()

    @pl.loop(0, RING * CHUNKS)
    def _(n):
        early = n < 2 * RING
        last = (n - 2 * RING) // 2
        turn = jnp.where(early, n % RING, jnp.where(last == 0, 2, jnp.where(last == RING - 1, 0, 2 * last - 1)))
        chunk = jnp.where(early, n // RING, 2 + n % 2)
        to = lax.rem(z + turn, RING)

        for at_step, arrivals, crossed, count in WAITS:
            @pl.when(n == at_step)
            def _(arrivals=arrivals, crossed=crossed, count=count):
                for d in arrivals:
                    received(d)
                for d in crossed:
                    from_core(d)
                flush(count)

        @pl.when(chunk == 0)
        def _():
            @pl.when(turn > 0)
            def _():
                remote(qbuf.at[turn], qbuf.at[turn], q_sem.at[0, turn], q_sem.at[1, turn], {"uly": to}).wait_recv()

            for g in range(GROUP):
                q = qbuf[turn, :, g * D:(g + 1) * D].astype(jnp.float32) * SCALE2
                high = q.astype(jnp.bfloat16)
                at = slice(g * rows, (g + 1) * rows)
                qcat[turn, at, :D] = high
                qcat[turn, at, D:] = (q - high.astype(jnp.float32)).astype(jnp.bfloat16)
            acc[turn] = jnp.zeros(acc.shape[1:], acc.dtype)

        qpos = column * COLUMN + c * UNIT + to * rows + lax.broadcasted_iota(jnp.int32, (1, rows), 1)
        qlow = jnp.zeros_like(qpos)
        for d in range(1, NDOC):
            qlow = jnp.where(starts[d:d + 1] <= qpos, jnp.maximum(qlow, starts[d:d + 1]), qlow)
        first = c * UNIT + to * rows + (CHUNKS - 1 - chunk) * CHUNK
        at = pl.ds(pl.multiple_of(first, 32), CHUNK)
        low = qlow - (column - REACH) * COLUMN - first
        kpos = lax.broadcasted_iota(jnp.int32, (CHUNK, rows), 0)
        allowed = (kpos - low).astype(jnp.uint32) <= (qpos - qlow).astype(jnp.uint32)
        k = kv[0, at]
        v = kv[1, at]
        kk = jnp.concatenate([k, k], axis=1)
        vv = jnp.concatenate([v, jnp.ones((CHUNK, ONES), v.dtype)], axis=1)
        p = jnp.exp2(contract(kk, qcat[turn], 1, 1))
        p = jnp.concatenate([jnp.where(allowed, p[:, g * rows:(g + 1) * rows], 0.0) for g in range(GROUP)], axis=1)
        acc[turn] += contract(vv, p.astype(jnp.bfloat16), 0, 0)

        @pl.when(chunk == CHUNKS - 1)
        def _():
            for g in range(GROUP):
                a = slice(g * rows, (g + 1) * rows)
                o = acc[turn, :D, a] / acc[turn, D:D + 1, a]
                obuf[turn, :, g * D:(g + 1) * D] = o.T.astype(jnp.bfloat16)

            @pl.when(turn == 0)
            def _():
                pltpu.make_async_copy(obuf.at[0], head(out, z, width), local_sem.at[5]).start()

            @pl.when(turn > 0)
            def _():
                remote(obuf.at[turn], head(out, z, width), o_sem.at[0], o_sem.at[1], {"uly": to}).start()

    for able, what in moves:
        @pl.when(able)
        def _(what=what):
            move(*what).wait_send()
    for d in range(REACH + 1):
        @pl.when(column >= d)
        def _(d=d):
            to_core(d).wait_send()
    for j in range(1, RING):
        remote(qbuf.at[j], qbuf.at[j], q_sem.at[0, j], q_sem.at[1, j], peer("uly", j)).wait_send()
    pltpu.make_async_copy(obuf.at[0], head(out, z, width), local_sem.at[5]).wait()
    got = obuf.at[pl.ds(1, RING - 1)]
    remote(got, got, o_sem.at[0], o_sem.at[1], peer("uly", 1)).wait()


def local(queries, keys, values, segments):
    rows, wide = queries.shape
    width = wide // RING
    M = GROUP * rows
    anywhere = pl.BlockSpec(memory_space=pl.ANY)
    vm = pl.BlockSpec(memory_space=pltpu.VMEM)
    out, stats = pl.pallas_call(
        ring_attend,
        out_shape=(
            jax.ShapeDtypeStruct((rows, wide), jnp.bfloat16),
            jax.ShapeDtypeStruct((1,), jnp.int32),
        ),
        in_specs=[vm, anywhere, anywhere, anywhere],
        out_specs=(anywhere, pl.BlockSpec(memory_space=pltpu.SMEM)),
        scratch_shapes=[
            pltpu.VMEM((2, (REACH + 1) * COLUMN, HEAD_SIZE), jnp.bfloat16),
            pltpu.VMEM((RING, rows, width), jnp.bfloat16),
            pltpu.VMEM((RING, rows, width), jnp.bfloat16),
            pltpu.VMEM((rows, wide), jnp.bfloat16),
            pltpu.VMEM((rows, RING * HEAD_SIZE), jnp.bfloat16),
            pltpu.VMEM((RING, M, 2 * HEAD_SIZE), jnp.bfloat16),
            pltpu.VMEM((RING, HEAD_SIZE + ONES, M), jnp.float32),
            pltpu.VMEM((3, 2 * RING, 2 * NDOC, rows), jnp.float32),
            pltpu.SemaphoreType.DMA((6,)),
            pltpu.SemaphoreType.DMA((2,)),
            pltpu.SemaphoreType.DMA((2, RING)),
            pltpu.SemaphoreType.DMA((2, 4)),
            pltpu.SemaphoreType.DMA((14,)),
            pltpu.SemaphoreType.DMA((REACH + 1,)),
            pltpu.SemaphoreType.DMA((REACH + 1,)),
            pltpu.SemaphoreType.DMA((REACH + 1,)),
            pltpu.SemaphoreType.DMA((2,)),
        ],
        compiler_params=pltpu.CompilerParams(collective_id=0, has_side_effects=True, vmem_limit_bytes=56 << 20),
        name="ring_attend",
    )(segments.reshape(1, rows), queries, keys, values)
    return lax.cond(stats[0] == 1, lambda *_: out, careful, queries, keys, values, segments)


def solution(mesh):
    split = Mesh(mesh.devices.reshape(4, 4, 2, mesh.shape["uly"]), AXES)
    return jax.shard_map(
        local,
        mesh=split,
        in_specs=(P(AXES, None), P(AXES, None), P(AXES, None), P(AXES)),
        out_specs=P(AXES, None),
        check_vma=False,
    )
```
